256 devices in a mesh: gx: 16 (over z_lo, y), gy: 16 (over x, z_hi, core).
Axes of the slice: x: 4, y: 4, z: 8 (z_hi: 2, z_lo: 4; z = z_hi * 4 + z_lo), core: 2. Of those that a mesh axis runs over, the one named last changes fastest.
Arguments:
- electric: float32 [3, 32, 512, 2048], P(None, None, 'gx', 'gy'), may hold values from -6 to 6
- magnetic: float32 [3, 32, 512, 2048], P(None, None, 'gx', 'gy'), may hold values from -6 to 6
- forward_field: float32 [3, 32, 512, 2048], P(None, None, 'gx', 'gy'), may hold values from -6 to 6
- material: int32 [32, 512, 2048], P(None, 'gx', 'gy'), may hold values from 0 to 3
- inv_permittivity: float32 [4], replicated, may hold values from 0.08 to 1
- spectral_rate: float32 [128], replicated, may hold values from 0.2 to 1.2
- intersection_partial: float32 [32, 512, 128], P('gx', 'gy'), may hold values from -0.3125 to 0.3125
- mode_profile: float32 [32, 32, 16384], P('gy', None, 'gx'), may hold values from -1 to 1
- sheet_offset: int32 [16], P('gy'), may hold values from 2 to 125
- plane_start: int32 [16], P('gy'), may hold values from 0 to 255
- monitor_length: int32 [16], P('gy'), may hold values from 128 to 256
Outputs:
- electric_out: float32 [3, 32, 512, 2048], P(None, None, 'gx', 'gy')
- magnetic_out: float32 [3, 32, 512, 2048], P(None, None, 'gx', 'gy')
- gradient: float32 [32, 512, 2048], P(None, 'gx', 'gy')
The draws below stay inside these ranges and needn't reach their ends.
All inputs are finite; a program needn't handle non-finite values.
Results may differ from the reference program's by a relative error of at most 0.0003.
Values sent between devices are 32-bit elements; how exact they have to be, the bound alone decides.
A program may use at most 192 MiB of HBM per device.

```python
import math
import jax
import jax.numpy as jnp
from jax import lax

CY = 128
NZ = 32
MODES = 32
FREQS = 128
SPAN_TICKS = 16
LABELS = 4
NX = 512
NY = 2048
PLANES = 16
N_GX = 16


def plant(result, own_key, least, largest):
    shape = result.shape
    index_at = [jax.random.randint(jax.random.fold_in(own_key, axis), (), 0, shape[axis]) for axis in range(len(shape))]
    result = result.at[tuple(index_at)].set(least)
    longest = shape.index(max(shape))
    index_at[longest] = (index_at[longest] + 1) % shape[longest]
    return result.at[tuple(index_at)].set(largest)


def levels(own_key, dims, split, smallest, top_value):
    loudness, own = 1.0, jax.random.fold_in(own_key, 6)
    for axis_at, blocks in split:
        steps = jnp.exp(jax.random.uniform(jax.random.fold_in(own, axis_at), (blocks,), jnp.float32, smallest / len(split), top_value / len(split)))
        loudness = loudness * jnp.repeat(steps, dims[axis_at] // blocks).reshape([-1 if axis == axis_at else 1 for axis in range(len(dims))])
    return loudness


def bell_draw(key, extent, spread, most, pieces=(), kind=jnp.bfloat16):
    result = spread * jax.random.normal(key, extent, jnp.float32)
    if pieces:
        result = result * levels(key, extent, pieces, -0.22, 0.18)
    return jnp.clip(result, -most, most).astype(kind)


def setup_inputs(seed: int = 0) -> dict:
    streams_of = jax.random.split(jax.random.key(seed), 12)
    return {
        "electric": bell_draw(streams_of[0], (3, NZ, NX, NY), 1.0, 6.0, ((2, 16), (3, 16)), jnp.float32),
        "magnetic": bell_draw(streams_of[1], (3, NZ, NX, NY), 1.0, 6.0, ((2, 16), (3, 16)), jnp.float32),
        "forward_field": bell_draw(streams_of[2], (3, NZ, NX, NY), 1.0, 6.0, ((2, 16), (3, 16)), jnp.float32),
        "material": plant(jax.random.randint(streams_of[3], (NZ, NX, NY), 0, LABELS), jax.random.fold_in(streams_of[3], 1), 0, LABELS - 1).astype(jnp.int32),
        "inv_permittivity": jnp.clip(jnp.exp(jax.random.uniform(streams_of[4], (LABELS,), jnp.float32, math.log(0.08), math.log(1.0))), 0.08, 1.0),
        "spectral_rate": jnp.clip(jax.random.uniform(streams_of[5], (FREQS,), jnp.float32, 0.2, 1.2), 0.2, 1.2),
        "intersection_partial": bell_draw(streams_of[6], (2 * N_GX, PLANES * MODES, FREQS), 0.02, 0.3125, ((0, 16), (1, 16)), jnp.float32),
        "mode_profile": bell_draw(streams_of[7], (2 * PLANES, MODES, NX * NZ), MODES ** -0.5, 1.0, ((0, 16), (2, 16)), jnp.float32),
        "sheet_offset": plant(jax.random.randint(streams_of[8], (PLANES,), 2, CY - 2), jax.random.fold_in(streams_of[8], 1), 2, (CY - 2) - 1).astype(jnp.int32),
        "plane_start": plant(jax.random.randint(streams_of[9], (PLANES,), 0, NX // 2), jax.random.fold_in(streams_of[9], 1), 0, (NX // 2) - 1).astype(jnp.int32),
        "monitor_length": plant(jax.random.randint(streams_of[10], (PLANES,), NX // 4, NX // 2 + 1), jax.random.fold_in(streams_of[10], 1), NX // 4, (NX // 2 + 1) - 1).astype(jnp.int32),
    }


COURANT = 0.5


def ahead(field, along_axis):
    size = field.shape[along_axis]
    rest = lax.slice_in_dim(field, 1, size, axis=along_axis)
    padding = jnp.zeros_like(lax.slice_in_dim(field, 0, 1, axis=along_axis))
    return jnp.concatenate([rest, padding], axis=along_axis)


def behind(field, along_axis):
    size = field.shape[along_axis]
    rest = lax.slice_in_dim(field, 0, size - 1, axis=along_axis)
    padding = jnp.zeros_like(lax.slice_in_dim(field, 0, 1, axis=along_axis))
    return jnp.concatenate([padding, rest], axis=along_axis)


def update_magnetic(electric, magnetic):
    electric_x, electric_field_y, electric_z = electric[0], electric[1], electric[2]
    magnetic_x = magnetic[0] - COURANT * ((ahead(electric_z, 2) - electric_z) - (ahead(electric_field_y, 0) - electric_field_y))
    magnetic_y = magnetic[1] - COURANT * ((ahead(electric_x, 0) - electric_x) - (ahead(electric_z, 1) - electric_z))
    magnetic_z = magnetic[2] - COURANT * ((ahead(electric_field_y, 1) - electric_field_y) - (ahead(electric_x, 2) - electric_x))
    return jnp.stack([magnetic_x, magnetic_y, magnetic_z])


def advance_displacement(electric, magnetic, coupling):
    magnetic_x, magnetic_y, magnetic_z = magnetic[0], magnetic[1], magnetic[2]
    electric_x = electric[0] + coupling * ((magnetic_z - behind(magnetic_z, 2)) - (magnetic_y - behind(magnetic_y, 0)))
    electric_field_y = electric[1] + coupling * ((magnetic_x - behind(magnetic_x, 0)) - (magnetic_z - behind(magnetic_z, 1)))
    electric_z = electric[2] + coupling * ((magnetic_y - behind(magnetic_y, 1)) - (magnetic_x - behind(magnetic_x, 2)))
    return jnp.stack([electric_x, electric_field_y, electric_z])


def reference(electric, magnetic, forward_field, material, inv_permittivity, spectral_rate, intersection_partial, mode_profile, sheet_offset, plane_start, monitor_length):
    highest = lax.Precision.HIGHEST
    coupling = COURANT * inv_permittivity[material]
    cotangent = jnp.sum(intersection_partial.reshape(N_GX, 2, PLANES, MODES, FREQS), axis=0)
    tick_moments = jnp.arange(SPAN_TICKS).astype(jnp.float32)
    rotation_radians = spectral_rate[:, None] * tick_moments[None, :]
    cosine_table = jnp.cos(rotation_radians)
    sine_table = jnp.sin(rotation_radians)
    coefficients = jnp.einsum("pmf,ft->pmt", cotangent[0], cosine_table, precision=highest) - jnp.einsum("pmf,ft->pmt", cotangent[1], sine_table, precision=highest)
    profile = mode_profile.reshape(PLANES, 2, MODES, NX, NZ)
    cells_x = jnp.arange(NX).astype(jnp.int32)
    first_cell = plane_start.astype(jnp.int32)
    final_cell = (plane_start + monitor_length).astype(jnp.int32)
    extent_mask = ((cells_x[None, :] >= first_cell[:, None]) & (cells_x[None, :] < final_cell[:, None])).astype(jnp.float32)
    current = jnp.einsum("pcmxz,pmt->pctzx", profile, coefficients, precision=highest) * extent_mask[:, None, None, None, :]
    plane_rows = (jnp.arange(PLANES).astype(jnp.int32) * CY + sheet_offset.astype(jnp.int32)).astype(jnp.int32)
    gradient = jnp.zeros((NZ, NX, NY), jnp.float32)
    for moment in range(SPAN_TICKS):
        magnetic = update_magnetic(electric, magnetic)
        electric = advance_displacement(electric, magnetic, coupling)
        current_now = current[:, :, moment]
        electric_x = electric[0].at[:, :, plane_rows].add(jnp.transpose(current_now[:, 0], (1, 2, 0)))
        electric_z = electric[2].at[:, :, plane_rows].add(jnp.transpose(current_now[:, 1], (1, 2, 0)))
        electric = jnp.stack([electric_x, electric[1], electric_z])
        gradient = gradient + jnp.sum(electric * forward_field, axis=0)
    return electric, magnetic, gradient / SPAN_TICKS
```

```python
import functools

import jax
import jax.numpy as jnp
from jax import lax
from jax.experimental import pallas as pl
from jax.experimental.pallas import tpu as pltpu
from jax.sharding import PartitionSpec as P

MESH = pl.DeviceIdType.MESH
TICKS = 16
K = 4
ROUNDS = TICKS // K
CH = 4
TILES = 5
TOP = 8
ROWS = 56
PAD = 5
HIGHEST = lax.Precision.HIGHEST

DIRS = ((-1, 0), (1, 0), (0, -1), (0, 1), (-1, -1), (1, -1), (-1, 1), (1, 1))
OPPOSITE = (1, 0, 3, 2, 7, 6, 5, 4)


def lanes_roll(v, shift):
    if isinstance(shift, int):
        shift = shift % 128
        return v if shift == 0 else pltpu.roll(v, shift, 1)
    return pltpu.roll(v, lax.rem(shift + 256, 128), 1)


def rows_roll(v, shift):
    return pltpu.roll(v, shift % 8, 0)


def tile_rows(xt):
    return pl.ds(TOP + 8 * xt, 8)


def kernel(
    n_gx, n_gy, nz,
    e_in, h_in, f_in, material_in, inverse, rate, partial, profile_in, offset, start, length,
    e_out, h_out, g_out,
    eh, coup, fwd, grad, labels, strip, strip_c, strip_j, own_pack,
    send_y, send_c, recv_x, recv_y, recv_c,
    w_send, w_all, profile, j_flat, j_all, j_now, v_send, v_recv, c_recv, inject_a, inject_b,
    load_sem, ssem, rsem, w_ssem, w_rsem, p_ssem, p_rsem, c_ssem, c_rsem, v_ssem, v_rsem,
):
    chunks = nz // CH
    gx = lax.axis_index("gx")
    gy = lax.axis_index("gy")
    f32 = jnp.float32
    lane = lax.broadcasted_iota(jnp.int32, (8, 128), 1)
    sub = lax.broadcasted_iota(jnp.int32, (8, 128), 0)
    group = lane // 8
    place = lane - group * 8
    low_half = place < 4
    zero = jnp.zeros((8, 128), f32)
    own_rows = pl.ds(TOP + 4, 32)

    exists = []
    devices = []
    for dx, dy in DIRS:
        ok = None
        for d, p, n in ((dx, gx, n_gx), (dy, gy, n_gy)):
            if d:
                here = (p > 0) if d < 0 else (p < n - 1)
                ok = here if ok is None else jnp.logical_and(ok, here)
        exists.append(ok)
        devices.append((gx + dx, gy + dy))

    def clear(zi, carry):
        for c in range(6):
            for row in (0, 8, 40, 48):
                eh[c, zi, pl.ds(row, 8), :] = zero
            strip[c, zi] = zero
        for row in (8, 40):
            labels[zi, pl.ds(row, 8), :] = jnp.full((8, 128), 4, jnp.int32)
            for c in range(3):
                fwd[c, zi, pl.ds(row, 8), :] = zero
        for xt in range(TILES):
            grad[zi, tile_rows(xt), :] = zero
            j_now[zi, pl.ds(8 * xt, 8), :] = zero
        strip_c[zi] = zero
        for c in range(2):
            strip_j[c, zi] = zero
        return carry

    lax.fori_loop(0, nz + 2 * PAD, clear, 0)
    for zi in [*range(PAD), *range(nz + PAD, nz + 2 * PAD)]:
        for row in range(16, 40, 8):
            for c in range(6):
                eh[c, zi, pl.ds(row, 8), :] = zero
            for c in range(3):
                fwd[c, zi, pl.ds(row, 8), :] = zero
        for xt in range(TILES):
            coup[zi, tile_rows(xt), :] = zero

    planes = pl.ds(PAD, nz)
    loads = [
        pltpu.make_async_copy(e_in, eh.at[pl.ds(0, 3), planes, own_rows, :], load_sem.at[1]),
        pltpu.make_async_copy(h_in, eh.at[pl.ds(3, 3), planes, own_rows, :], load_sem.at[2]),
        pltpu.make_async_copy(material_in, labels.at[planes, own_rows, :], load_sem.at[3]),
        pltpu.make_async_copy(profile_in, profile.at[:, pl.ds(4 * nz, 32 * nz)], load_sem.at[4]),
        pltpu.make_async_copy(f_in, fwd.at[:, planes, own_rows, :], load_sem.at[5]),
    ]
    for load in loads:
        load.start()

    def clear_received(z, carry):
        for par in range(2):
            for c in range(6):
                recv_x[par, c, z] = zero
            for d in range(2):
                recv_y[par, d, z] = zero
        for d in range(2):
            v_recv[d, z] = zero
        c_recv[z] = zero
        return carry

    lax.fori_loop(0, nz, clear_received, 0)
    for q in range(chunks):
        for par in range(2):
            for d in range(2):
                recv_c[par, d, q] = zero
    for m in range(8):
        profile[pl.ds(8 * m, 8), pl.ds(0, 4 * nz)] = jnp.zeros((8, 4 * nz), f32)
        profile[pl.ds(8 * m, 8), pl.ds(36 * nz, 4 * nz)] = jnp.zeros((8, 4 * nz), f32)

    barrier = pltpu.get_barrier_semaphore()
    for j in range(1, n_gx):
        peer = (lax.rem(gx + j, n_gx), gy)
        pl.semaphore_signal(barrier, inc=1, device_id=peer, device_id_type=MESH)
    for d in range(2, 8):
        @pl.when(exists[d])
        def _():
            pl.semaphore_signal(barrier, inc=1, device_id=devices[d], device_id_type=MESH)
    one = lambda flag: jnp.where(flag, 1, 0)
    near_x = one(exists[0]) + one(exists[1])
    near_y = one(exists[2]) + one(exists[3])
    pl.semaphore_wait(barrier, n_gx - 1 + near_y * (1 + near_x))

    def remote(src, dst, send, recv, d):
        return pltpu.make_async_remote_copy(
            src_ref=src, dst_ref=dst, send_sem=send, recv_sem=recv,
            device_id=devices[d], device_id_type=MESH,
        )

    def start_if(d, copy):
        @pl.when(exists[d])
        def _():
            copy.start()

    def wait_if(d, copy):
        @pl.when(exists[d])
        def _():
            copy.wait()

    row = lax.broadcasted_iota(jnp.int32, (32, 128), 0)
    tick = (4 * (row - (row // 4) * 4) + row // 8).astype(f32)
    radians = tick * rate[...]
    cosine = jnp.cos(radians)
    sine = jnp.sin(radians)
    cosine = jnp.concatenate([cosine] * 4, axis=0)
    sine = jnp.concatenate([sine] * 4, axis=0)
    dims = (((1,), (1,)), ((), ()))
    term = lax.dot_general(partial[0], cosine, dims, precision=HIGHEST, preferred_element_type=f32)
    term = term - lax.dot_general(
        partial[1], sine, dims, precision=HIGHEST, preferred_element_type=f32
    )
    packed = zero
    for g in range(4):
        packed = jnp.where(lane // 32 == g, term[8 * g : 8 * g + 8], packed)
    w_send[...] = packed

    def w_copy(j, slot, sem_slot):
        peer = (lax.rem(gx + j, n_gx), gy)
        return pltpu.make_async_remote_copy(
            src_ref=w_send, dst_ref=w_all.at[slot], send_sem=w_ssem.at[sem_slot],
            recv_sem=w_rsem.at[sem_slot], device_id=peer, device_id_type=MESH,
        )

    for j in range(1, n_gx):
        w_copy(j, j, j).start()

    def p_copy(d):
        src = profile_in.at[:, pl.ds(0 if d == 0 else 28 * nz, 4 * nz)]
        dst = profile.at[:, pl.ds(36 * nz if d == 0 else 0, 4 * nz)]
        return remote(src, dst, p_ssem.at[d], p_rsem.at[OPPOSITE[d]], d)

    def p_wait(d):
        src = profile_in.at[:, pl.ds(0, 4 * nz)]
        dst = profile.at[:, pl.ds(0 if d == 0 else 36 * nz, 4 * nz)]
        return remote(src, dst, p_ssem.at[d], p_rsem.at[d], d)

    for d in range(2):
        start_if(d, p_copy(d))

    def message(d, q, par, arriving):
        z0 = pl.multiple_of(q * CH, CH)
        zs = pl.ds(z0, CH)
        sem = rsem.at[par, d if arriving else OPPOSITE[d], q]
        if d < 2:
            lower = (d == 0) == arriving
            dst = recv_x.at[par, :, zs, pl.ds(0 if lower else 4, 4), :]
            src = eh.at[:, pl.ds(z0 + PAD, CH), pl.ds(TOP + 4 if d == 0 else TOP + 32, 4), :]
        elif d < 4:
            dst = recv_y.at[par, (d - 2) if arriving else (3 - d), zs]
            src = send_y.at[d - 2, zs]
        else:
            side = (d - 4) // 2
            dx = DIRS[d][0]
            out = pl.ds(4 if dx < 0 else 0, 4)
            into = pl.ds(4 if (dx > 0) == arriving else 0, 4)
            dst = recv_c.at[par, side if arriving else 1 - side, q, into, :]
            src = send_c.at[side, q, out, :]
        return remote(src, dst, ssem.at[d, q], sem, d)

    def pack_and_send(q, par):
        corner = [zero, zero]
        for i in range(CH):
            z = q * CH + i
            zi = z + PAD
            packs = []
            for half in range(2):
                acc = zero
                for c in range(3):
                    for xt in range(TILES):
                        v = eh[3 * half + c, zi, tile_rows(xt), :]
                        acc = jnp.where(
                            group == 5 * c + xt, lanes_roll(v, 40 * c + 8 * xt + 4), acc
                        )
                own_pack[half, z] = acc
                packs.append(acc)
            pe, ph = packs
            down = jnp.where(low_half, lanes_roll(ph, -4), pe)
            up = jnp.where(low_half, pe, lanes_roll(ph, 4))
            for side, v in ((0, down), (1, up)):
                send_y[side, z] = v
                moved = jnp.where(sub < 4, lanes_roll(v, 8 * i - 32), lanes_roll(v, 8 * i))
                here = (group == i) | (group == 5 + i) | (group == 10 + i)
                corner[side] = jnp.where(here, moved, corner[side])
        for side in range(2):
            send_c[side, q] = corner[side]
        for d in range(8):
            start_if(d, message(d, q, par, False))

    xt0 = ((group == 0) | (group == 5) | (group == 10)) & (sub < 4)
    xt4 = ((group == 4) | (group == 9) | (group == 14)) & (sub >= 4)

    def unpack(q, par, r):
        for i in range(CH):
            z = q * CH + i
            zi = z + PAD
            packs = []
            for half in range(2):
                acc = own_pack[half, z]
                for c in range(3):
                    v = recv_x[par, 3 * half + c, z]
                    old = eh[3 * half + c, zi, tile_rows(0), :]
                    eh[3 * half + c, zi, tile_rows(0), :] = jnp.where(sub < 4, v, old)
                    old = eh[3 * half + c, zi, tile_rows(4), :]
                    eh[3 * half + c, zi, tile_rows(4), :] = jnp.where(sub < 4, old, v)
                    acc = jnp.where((group == 5 * c) & (sub < 4), lanes_roll(v, 40 * c + 4), acc)
                    acc = jnp.where(
                        (group == 5 * c + 4) & (sub >= 4), lanes_roll(v, 40 * c + 36), acc
                    )
                packs.append(acc)
            pe, ph = packs
            sides = []
            for side in range(2):
                v = recv_y[par, side, z]
                x = recv_c[par, side, q]
                v = jnp.where(xt0, lanes_roll(x, -8 * i), v)
                v = jnp.where(xt4, lanes_roll(x, 32 - 8 * i), v)
                sides.append(v)
            from_down, from_up = sides
            right = (
                jnp.where(low_half, pe, from_up),
                jnp.where(low_half, ph, lanes_roll(from_up, 4)),
            )
            left = (
                jnp.where(low_half, from_down, pe),
                jnp.where(low_half, lanes_roll(from_down, -4), ph),
            )
            for half in range(2):
                for c in range(3):
                    strip[3 * half + c, zi] = jnp.where(
                        lane < 64,
                        lanes_roll(right[half], -40 * c),
                        lanes_roll(left[half], 64 - 40 * c),
                    )
            for xt in range(TILES):
                j_now[zi, pl.ds(8 * xt, 8), :] = lanes_roll(j_all[z, pl.ds(8 * xt, 8), :], -r)
            for c in range(2):
                a = lanes_roll(inject_a[z], 6 - 4 * c - r)
                b = lanes_roll(inject_b[z], 1 - 4 * c - r)
                strip_j[c, zi] = jnp.where(place == 6, a, jnp.where(place == 1, b, zero))

    loads[0].wait()
    loads[1].wait()

    def first_chunk(q, carry):
        pack_and_send(q, 0)
        return carry

    lax.fori_loop(0, chunks, first_chunk, 0)

    loads[2].wait()

    def couple(z, carry):
        zi = z + PAD
        for xt in range(TILES):
            label = labels[zi, tile_rows(xt), :]
            value = zero
            for n in range(4):
                value = jnp.where(label == n, 0.5 * inverse[n], value)
            coup[zi, tile_rows(xt), :] = value
        return carry

    lax.fori_loop(0, nz, couple, 0)

    def c_copy(d, arriving):
        lower = (d == 0) == arriving
        src = coup.at[planes, pl.ds(TOP + 4 if d == 0 else TOP + 32, 4), :]
        dst = c_recv.at[:, pl.ds(0 if lower else 4, 4), :]
        return remote(src, dst, c_ssem.at[d], c_rsem.at[d if arriving else OPPOSITE[d]], d)

    for d in range(2):
        start_if(d, c_copy(d, False))

    total = w_send[...]
    for j in range(1, n_gx):
        w_copy(j, j, j).wait()
        total = total + w_all[j]
    loads[3].wait()
    for d in range(2):
        @pl.when(exists[d])
        def _():
            p_copy(d).wait_send()
            p_wait(d).wait_recv()
    parts = []
    for c in range(2):
        for g in range(4):
            keep = (lane < 32) & (lax.rem(lane // 4, 2) == c)
            parts.append(jnp.where(keep, lanes_roll(total, -32 * g), zero))
    weights = jnp.concatenate(parts, axis=0)
    first = start[0]
    last = start[0] + length[0]
    for xt in range(TILES):
        cells = pl.ds(8 * nz * xt, 8 * nz)
        now = lax.dot_general(
            profile[:, cells], weights, (((0,), (0,)), ((), ())),
            precision=HIGHEST, preferred_element_type=f32,
        )
        x = gx * 32 - 4 + 8 * xt + lax.broadcasted_iota(jnp.int32, (8 * nz, 128), 0) // nz
        j_flat[cells, :] = jnp.where((x >= first) & (x < last), now, 0.0)

    for d in range(2):
        wait_if(d, c_copy(d, True))
    where_at = offset[0]

    def prepare(z, carry):
        zi = z + PAD
        halo = c_recv[z]
        coup[zi, tile_rows(0), :] = jnp.where(sub < 4, halo, coup[zi, tile_rows(0), :])
        coup[zi, tile_rows(4), :] = jnp.where(sub < 4, coup[zi, tile_rows(4), :], halo)
        acc = zero
        for xt in range(TILES):
            v = coup[zi, tile_rows(xt), :]
            acc = jnp.where(group == xt, lanes_roll(v, 8 * xt + 4), acc)
            j = j_flat[pl.ds(z + 8 * nz * xt, 8, stride=nz), :]
            j_all[z, pl.ds(8 * xt, 8), :] = j
            acc = jnp.where(group == 5 + xt, lanes_roll(j, 40 + 8 * xt), acc)
        v_send[0, z] = jnp.where((lane >= 40) & (where_at != 2), 0.0, acc)
        v_send[1, z] = jnp.where((lane >= 40) & (where_at != 125), 0.0, acc)
        return carry

    lax.fori_loop(0, nz, prepare, 0)

    def v_copy(d, arriving):
        return remote(
            v_send.at[d - 2], v_recv.at[(d - 2) if arriving else (3 - d)],
            v_ssem.at[d - 2], v_rsem.at[(d - 2) if arriving else (3 - d)], d,
        )

    for d in (2, 3):
        start_if(d, v_copy(d, False))
    for d in (2, 3):
        wait_if(d, v_copy(d, True))

    def finish(z, carry):
        zi = z + PAD
        own_down, own_up = v_send[0, z], v_send[1, z]
        from_down, from_up = v_recv[0, z], v_recv[1, z]
        right = jnp.where(low_half, own_up, from_up)
        left = jnp.where(low_half, from_down, own_up)
        strip_c[zi] = jnp.where(lane < 64, right, lanes_roll(left, 64))
        inject_a[z] = jnp.where(lane < 64, lanes_roll(from_up, -40), lanes_roll(own_down, 24))
        inject_b[z] = jnp.where(lane < 64, lanes_roll(own_up, -40), lanes_roll(from_down, 24))
        return carry

    lax.fori_loop(0, nz, finish, 0)
    loads[4].wait()

    half = jnp.full((8, 128), 0.5, f32)
    outside_x = (sub < 4) & (gx == 0)
    half_first = jnp.where(outside_x, 0.0, half)
    outside = (outside_x & ((group == 0) | (group == 8))) | (
        (lane >= 64) & low_half & (gy == 0)
    )
    half_strip = jnp.where(outside, 0.0, half)
    on_sheet = lane == where_at

    def up_rows(v):
        return rows_roll(jnp.where(sub == 0, lanes_roll(v, -8), v), -1)

    def down_rows(v):
        return rows_roll(jnp.where(sub == 7, lanes_roll(v, 8), v), 1)

    def plane_step(z, s):
        zi = z + PAD
        inside = z >= 0
        k_strip = jnp.where(inside, half_strip, 0.0)
        k_first = jnp.where(inside, half_first, 0.0)
        k_rest = jnp.where(inside, half, 0.0)
        sx, sy, sz, tx, ty, tz = [strip[c, zi] for c in range(6)]
        sx_up, sy_up = strip[0, zi + 1], strip[1, zi + 1]
        tx_dn, ty_dn = strip[3, zi - 1], strip[4, zi - 1]
        ux = tx - k_strip * ((lanes_roll(sz, -1) - sz) - (sy_up - sy))
        uy = ty - k_strip * ((sx_up - sx) - (up_rows(sz) - sz))
        uz = tz - k_strip * ((up_rows(sy) - sy) - (lanes_roll(sx, -1) - sx))
        c = strip_c[zi]
        vx = sx + c * ((uz - lanes_roll(uz, 1)) - (uy - ty_dn))
        vy = sy + c * ((ux - tx_dn) - (uz - down_rows(uz)))
        vz = sz + c * ((uy - down_rows(uy)) - (ux - lanes_roll(ux, 1)))
        if s == 0:
            vx = vx + strip_j[0, zi]
            vz = vz + strip_j[1, zi]
        for n, v in enumerate((vx, vy, vz, ux, uy, uz)):
            strip[n, zi] = v
        for xt in range(TILES):
            rows = tile_rows(xt)
            above = pl.ds(TOP + 8 * xt + 1, 8)
            below = pl.ds(TOP + 8 * xt - 1, 8)
            k = k_first if xt == 0 else k_rest
            ex, ey, ez = [eh[n, zi, rows, :] for n in range(3)]
            hx, hy, hz = [eh[n, zi, rows, :] for n in range(3, 6)]
            ex_up, ey_up = eh[0, zi + 1, rows, :], eh[1, zi + 1, rows, :]
            ey_x, ez_x = eh[1, zi, above, :], eh[2, zi, above, :]
            turn = 127 - (8 * xt + 4)
            ex_y = jnp.where(lane == 127, lanes_roll(sx, turn), lanes_roll(ex, -1))
            ez_y = jnp.where(lane == 127, lanes_roll(sz, turn), lanes_roll(ez, -1))
            hx = hx - k * ((ez_y - ez) - (ey_up - ey))
            hy = hy - k * ((ex_up - ex) - (ez_x - ez))
            hz = hz - k * ((ey_x - ey) - (ex_y - ex))
            eh[3, zi, rows, :] = hx
            eh[4, zi, rows, :] = hy
            eh[5, zi, rows, :] = hz
            hx_dn, hy_dn = eh[3, zi - 1, rows, :], eh[4, zi - 1, rows, :]
            hy_x, hz_x = eh[4, zi, below, :], eh[5, zi, below, :]
            turn = -(64 + 8 * xt + 3)
            hx_y = jnp.where(lane == 0, lanes_roll(ux, turn), lanes_roll(hx, 1))
            hz_y = jnp.where(lane == 0, lanes_roll(uz, turn), lanes_roll(hz, 1))
            cc = coup[zi, rows, :]
            jx = jnp.broadcast_to(j_now[zi, pl.ds(8 * xt, 8), pl.ds(8 * s, 1)], (8, 128))
            jz = jnp.broadcast_to(j_now[zi, pl.ds(8 * xt, 8), pl.ds(8 * s + 4, 1)], (8, 128))
            ex = ex + cc * ((hz - hz_y) - (hy - hy_dn)) + jnp.where(on_sheet, jx, 0.0)
            ey = ey + cc * ((hx - hx_dn) - (hz - hz_x))
            ez = ez + cc * ((hy - hy_x) - (hx - hx_y)) + jnp.where(on_sheet, jz, 0.0)
            eh[0, zi, rows, :] = ex
            eh[1, zi, rows, :] = ey
            eh[2, zi, rows, :] = ez
            grad[zi, rows, :] = grad[zi, rows, :] + (
                ex * fwd[0, zi, rows, :] + ey * fwd[1, zi, rows, :] + ez * fwd[2, zi, rows, :]
            )

    def one_round(r, carry):
        par = lax.rem(r, 2)
        later = lax.rem(r + 1, 2)

        def one_chunk(q, carry):
            @pl.when(q < chunks)
            def _():
                for d in range(8):
                    wait_if(d, message(d, q, par, True))
                unpack(q, par, r)

            def wave(i, carry):
                w = q * CH - 1 + i
                for s in range(K):
                    plane_step(w - s, s)
                return carry

            lax.fori_loop(0, CH, wave, 0)

            @pl.when(jnp.logical_and(q > 0, r < ROUNDS - 1))
            def _():
                pack_and_send(q - 1, later)

            return carry

        return lax.fori_loop(0, chunks + 1, one_chunk, carry)

    lax.fori_loop(0, ROUNDS, one_round, 0)

    stores = [
        pltpu.make_async_copy(eh.at[pl.ds(0, 3), planes, own_rows, :], e_out, load_sem.at[1]),
        pltpu.make_async_copy(eh.at[pl.ds(3, 3), planes, own_rows, :], h_out, load_sem.at[2]),
        pltpu.make_async_copy(grad.at[planes, own_rows, :], g_out, load_sem.at[3]),
    ]
    for store in stores:
        store.start()
    for store in stores:
        store.wait()


def shards(n_gx, n_gy, *args):
    (electric, magnetic, forward_field, material, inv_permittivity, spectral_rate,
     intersection_partial, mode_profile, sheet_offset, plane_start, monitor_length) = args
    nz = electric.shape[1]
    f32 = jnp.float32
    zp = nz + 2 * PAD
    chunks = nz // CH
    dma = pltpu.SemaphoreType.DMA
    vmem = lambda *shape: pltpu.VMEM(shape, f32)
    anyspace = pl.BlockSpec(memory_space=pl.ANY)
    smem = pl.BlockSpec(memory_space=pltpu.SMEM)
    vm = pl.BlockSpec(memory_space=pltpu.VMEM)
    e, h, g = pl.pallas_call(
        functools.partial(kernel, n_gx, n_gy, nz),
        out_shape=[
            jax.ShapeDtypeStruct(electric.shape, f32),
            jax.ShapeDtypeStruct(electric.shape, f32),
            jax.ShapeDtypeStruct(material.shape, f32),
        ],
        in_specs=[anyspace, anyspace, anyspace, anyspace, smem, vm, vm, anyspace, smem, smem, smem],
        out_specs=[anyspace] * 3,
        scratch_shapes=[
            vmem(6, zp, ROWS, 128),
            vmem(zp, ROWS, 128),
            vmem(3, zp, ROWS, 128),
            vmem(zp, ROWS, 128),
            pltpu.VMEM((zp, ROWS, 128), jnp.int32),
            vmem(6, zp, 8, 128),
            vmem(zp, 8, 128),
            vmem(2, zp, 8, 128),
            vmem(2, nz, 8, 128),
            vmem(2, nz, 8, 128),
            vmem(2, chunks, 8, 128),
            vmem(2, 6, nz, 8, 128),
            vmem(2, 2, nz, 8, 128),
            vmem(2, 2, chunks, 8, 128),
            vmem(8, 128),
            vmem(n_gx, 8, 128),
            vmem(64, 40 * nz),
            vmem(40 * nz, 128),
            vmem(nz, 40, 128),
            vmem(zp, 40, 128),
            vmem(2, nz, 8, 128),
            vmem(2, nz, 8, 128),
            vmem(nz, 8, 128),
            vmem(nz, 8, 128),
            vmem(nz, 8, 128),
            dma((6,)),
            dma((8, chunks)),
            dma((2, 8, chunks)),
            dma((n_gx,)),
            dma((n_gx,)),
            dma((2,)),
            dma((2,)),
            dma((2,)),
            dma((2,)),
            dma((2,)),
            dma((2,)),
        ],
        compiler_params=pltpu.CompilerParams(
            collective_id=0, has_side_effects=True, vmem_limit_bytes=56 << 20
        ),
    )(
        electric, magnetic, forward_field, material, inv_permittivity,
        spectral_rate.reshape(1, -1), intersection_partial,
        mode_profile.reshape(-1, mode_profile.shape[2]),
        sheet_offset, plane_start, monitor_length,
    )
    return e, h, g * (1.0 / TICKS)


def solution(mesh):
    placed = (
        P(None, None, "gx", "gy"),
        P(None, None, "gx", "gy"),
        P(None, None, "gx", "gy"),
        P(None, "gx", "gy"),
        P(),
        P(),
        P("gx", "gy", None),
        P("gy", None, "gx"),
        P("gy"),
        P("gy"),
        P("gy"),
    )
    return jax.shard_map(
        functools.partial(shards, mesh.shape["gx"], mesh.shape["gy"]),
        mesh=mesh,
        in_specs=placed,
        out_specs=(P(None, None, "gx", "gy"), P(None, None, "gx", "gy"), P(None, "gx", "gy")),
        check_vma=False,
    )
```

```python
import functools

import jax
import jax.numpy as jnp
from jax import lax
from jax.experimental import pallas as pl
from jax.experimental.pallas import tpu as pltpu
from jax.sharding import PartitionSpec as P

MESH = pl.DeviceIdType.MESH
TICKS = 16
K = 4
ROUNDS = TICKS // K
CH = 4
TILES = 5
TOP = 8
ROWS = 56
PAD = 1
EXTRA = 5
HIGHEST = lax.Precision.HIGHEST

DIRS = ((-1, 0), (1, 0), (0, -1), (0, 1), (-1, -1), (1, -1), (-1, 1), (1, 1))
OPPOSITE = (1, 0, 3, 2, 7, 6, 5, 4)


def lanes_roll(v, shift):
    if isinstance(shift, int):
        shift = shift % 128
        return v if shift == 0 else pltpu.roll(v, shift, 1)
    return pltpu.roll(v, lax.rem(shift + 256, 128), 1)


def rows_roll(v, shift):
    return pltpu.roll(v, shift % 8, 0)


def tile_rows(xt):
    return pl.ds(TOP + 8 * xt, 8)


def kernel(
    n_gx, n_gy, nz,
    e_in, h_in, f_in, material_in, inverse, rate, partial, profile_in, offset, start, length,
    e_out, h_out, g_out,
    eh, e0, h0, e1, h1, e2, h2, e3, h3, strip0, strip1, strip2, strip3,
    grad0, grad1, grad2, grad3, coup, fwd, labels, strip_c, strip_j, own_pack,
    send_y, send_c, recv_x, recv_y, recv_c,
    w_send, w_all, profile, j_flat, j_all, pick, v_send, v_recv, c_recv, inject_a, inject_b,
    load_sem, out_sem, ssem, rsem, w_ssem, w_rsem, p_ssem, p_rsem, c_ssem, c_rsem, v_ssem, v_rsem,
):
    chunks = nz // CH
    gx = lax.axis_index("gx")
    gy = lax.axis_index("gy")
    f32 = jnp.float32
    lane = lax.broadcasted_iota(jnp.int32, (8, 128), 1)
    sub = lax.broadcasted_iota(jnp.int32, (8, 128), 0)
    group = lane // 8
    place = lane - group * 8
    low_half = place < 4
    zero = jnp.zeros((8, 128), f32)
    own_rows = pl.ds(TOP + 4, 32)

    exists = []
    devices = []
    for dx, dy in DIRS:
        ok = None
        for d, p, n in ((dx, gx, n_gx), (dy, gy, n_gy)):
            if d:
                here = (p > 0) if d < 0 else (p < n - 1)
                ok = here if ok is None else jnp.logical_and(ok, here)
        exists.append(ok)
        devices.append((gx + dx, gy + dy))

    e_at = (e0, e1, e2, e3)
    h_at = (h0, h1, h2, h3, eh)
    strip_at = (strip0, strip1, strip2, strip3)
    grads = (grad0, grad1, grad2, grad3)

    planes = pl.ds(PAD, nz)
    loads = [
        pltpu.make_async_copy(e_in, eh.at[pl.ds(0, 3), planes, own_rows, :], load_sem.at[1]),
        pltpu.make_async_copy(h_in, eh.at[pl.ds(3, 3), planes, own_rows, :], load_sem.at[2]),
        pltpu.make_async_copy(material_in, labels.at[planes, own_rows, :], load_sem.at[3]),
        pltpu.make_async_copy(profile_in, profile.at[:, pl.ds(4 * nz, 32 * nz)], load_sem.at[4]),
        pltpu.make_async_copy(f_in, fwd.at[:, planes, own_rows, :], load_sem.at[5]),
    ]
    for load in loads:
        load.start()

    for c in range(3):
        for xt in range(TILES):
            eh[3 + c, 0, tile_rows(xt), :] = zero
    for level in range(K):
        for c in range(3):
            for xt in range(TILES):
                h_at[level][c, 0, tile_rows(xt), :] = zero
                e_at[level][c, nz + PAD, tile_rows(xt), :] = zero
            strip_at[level][3 + c, 0] = zero
            strip_at[level][c, nz + PAD] = zero

    def clear(zi, carry):
        for total in grads:
            for xt in range(TILES):
                total[zi, tile_rows(xt), :] = zero
        return carry

    lax.fori_loop(PAD, nz + PAD, clear, 0)

    def clear_x(side):
        rows = pl.ds(4 * side, 4)
        none = jnp.zeros((4, 128), f32)

        def at(z, carry):
            for par in range(2):
                for c in range(6):
                    recv_x[par, c, z, rows, :] = none
            c_recv[z, rows, :] = none
            return carry

        lax.fori_loop(0, nz, at, 0)
        edge = jnp.zeros((64, 4 * nz), f32)
        profile[:, pl.ds(36 * nz * side, 4 * nz)] = edge

    def clear_y(side):
        def at(z, carry):
            for par in range(2):
                recv_y[par, side, z] = zero
            v_recv[side, z] = zero
            return carry

        lax.fori_loop(0, nz, at, 0)

    for side in range(2):
        @pl.when(jnp.logical_not(exists[side]))
        def _():
            clear_x(side)

        @pl.when(jnp.logical_not(exists[2 + side]))
        def _():
            clear_y(side)

    for d in range(4, 8):
        rows = pl.ds(4 if DIRS[d][0] > 0 else 0, 4)

        @pl.when(jnp.logical_not(exists[d]))
        def _():
            for par in range(2):
                for q in range(chunks):
                    recv_c[par, (d - 4) // 2, q, rows, :] = jnp.zeros((4, 128), f32)

    barrier = pltpu.get_barrier_semaphore()
    for j in range(1, n_gx):
        peer = (lax.rem(gx + j, n_gx), gy)
        pl.semaphore_signal(barrier, inc=1, device_id=peer, device_id_type=MESH)
    for d in range(2, 8):
        @pl.when(exists[d])
        def _():
            pl.semaphore_signal(barrier, inc=1, device_id=devices[d], device_id_type=MESH)
    one = lambda flag: jnp.where(flag, 1, 0)
    near_x = one(exists[0]) + one(exists[1])
    near_y = one(exists[2]) + one(exists[3])
    pl.semaphore_wait(barrier, n_gx - 1 + near_y * (1 + near_x))

    def remote(src, dst, send, recv, d):
        return pltpu.make_async_remote_copy(
            src_ref=src, dst_ref=dst, send_sem=send, recv_sem=recv,
            device_id=devices[d], device_id_type=MESH,
        )

    def start_if(d, copy):
        @pl.when(exists[d])
        def _():
            copy.start()

    def wait_if(d, copy):
        @pl.when(exists[d])
        def _():
            copy.wait()

    row = lax.broadcasted_iota(jnp.int32, (32, 128), 0)
    tick = (4 * (row - (row // 4) * 4) + row // 8).astype(f32)
    radians = tick * rate[...]
    cosine = jnp.cos(radians)
    sine = jnp.sin(radians)
    cosine = jnp.concatenate([cosine] * 4, axis=0)
    sine = jnp.concatenate([sine] * 4, axis=0)
    dims = (((1,), (1,)), ((), ()))
    term = lax.dot_general(partial[0], cosine, dims, precision=HIGHEST, preferred_element_type=f32)
    term = term - lax.dot_general(
        partial[1], sine, dims, precision=HIGHEST, preferred_element_type=f32
    )
    packed = zero
    for g in range(4):
        packed = jnp.where(lane // 32 == g, term[8 * g : 8 * g + 8], packed)
    w_send[...] = packed

    def w_copy(j, slot, sem_slot):
        peer = (lax.rem(gx + j, n_gx), gy)
        return pltpu.make_async_remote_copy(
            src_ref=w_send, dst_ref=w_all.at[slot], send_sem=w_ssem.at[sem_slot],
            recv_sem=w_rsem.at[sem_slot], device_id=peer, device_id_type=MESH,
        )

    for j in range(1, n_gx):
        w_copy(j, j, j).start()

    def p_copy(d):
        src = profile_in.at[:, pl.ds(0 if d == 0 else 28 * nz, 4 * nz)]
        dst = profile.at[:, pl.ds(36 * nz if d == 0 else 0, 4 * nz)]
        return remote(src, dst, p_ssem.at[d], p_rsem.at[OPPOSITE[d]], d)

    def p_wait(d):
        src = profile_in.at[:, pl.ds(0, 4 * nz)]
        dst = profile.at[:, pl.ds(0 if d == 0 else 36 * nz, 4 * nz)]
        return remote(src, dst, p_ssem.at[d], p_rsem.at[d], d)

    for d in range(2):
        start_if(d, p_copy(d))

    def message(d, q, par, arriving):
        z0 = pl.multiple_of(q * CH, CH)
        zs = pl.ds(z0, CH)
        sem = rsem.at[par, d if arriving else OPPOSITE[d], q]
        if d < 2:
            lower = (d == 0) == arriving
            dst = recv_x.at[par, :, zs, pl.ds(0 if lower else 4, 4), :]
            src = eh.at[:, pl.ds(z0 + PAD, CH), pl.ds(TOP + 4 if d == 0 else TOP + 32, 4), :]
        elif d < 4:
            dst = recv_y.at[par, (d - 2) if arriving else (3 - d), zs]
            src = send_y.at[d - 2, zs]
        else:
            side = (d - 4) // 2
            dx = DIRS[d][0]
            out = pl.ds(4 if dx < 0 else 0, 4)
            into = pl.ds(4 if (dx > 0) == arriving else 0, 4)
            dst = recv_c.at[par, side if arriving else 1 - side, q, into, :]
            src = send_c.at[side, q, out, :]
        return remote(src, dst, ssem.at[d, q], sem, d)

    def pack(z, zi, slot):
        i = lax.rem(z, CH)
        packs = []
        for half in range(2):
            acc = zero
            for c in range(3):
                for xt in range(TILES):
                    v = eh[3 * half + c, zi, tile_rows(xt), :]
                    acc = jnp.where(
                        group == 5 * c + xt, lanes_roll(v, 40 * c + 8 * xt + 4), acc
                    )
            own_pack[half, slot] = acc
            packs.append(acc)
        pe, ph = packs
        down = jnp.where(low_half, lanes_roll(ph, -4), pe)
        up = jnp.where(low_half, pe, lanes_roll(ph, 4))
        here = (group == i) | (group == 5 + i) | (group == 10 + i)
        for side, v in ((0, down), (1, up)):
            send_y[side, slot] = v
            moved = jnp.where(sub < 4, lanes_roll(v, 8 * i + 96), lanes_roll(v, 8 * i))
            q = slot // CH
            send_c[side, q] = jnp.where(here, moved, send_c[side, q])

    def send(q, par):
        for d in range(8):
            start_if(d, message(d, q, par, False))

    xt0 = ((group == 0) | (group == 5) | (group == 10)) & (sub < 4)
    xt4 = ((group == 4) | (group == 9) | (group == 14)) & (sub >= 4)

    def unpack(z, zi, par, r):
        i = lax.rem(z, CH)
        q = z // CH
        packs = []
        for half in range(2):
            acc = own_pack[half, z]
            for c in range(3):
                v = recv_x[par, 3 * half + c, z]
                new = (e0, h0)[half]
                for xt in range(TILES):
                    old = eh[3 * half + c, z + PAD, tile_rows(xt), :]
                    if xt == 0:
                        old = jnp.where(sub < 4, v, old)
                    elif xt == 4:
                        old = jnp.where(sub < 4, old, v)
                    new[c, zi, tile_rows(xt), :] = old
                acc = jnp.where((group == 5 * c) & (sub < 4), lanes_roll(v, 40 * c + 4), acc)
                acc = jnp.where(
                    (group == 5 * c + 4) & (sub >= 4), lanes_roll(v, 40 * c + 36), acc
                )
            packs.append(acc)
        pe, ph = packs
        sides = []
        for side in range(2):
            v = recv_y[par, side, z]
            x = recv_c[par, side, q]
            v = jnp.where(xt0, lanes_roll(x, 128 - 8 * i), v)
            v = jnp.where(xt4, lanes_roll(x, 32 - 8 * i), v)
            sides.append(v)
        from_down, from_up = sides
        right = (
            jnp.where(low_half, pe, from_up),
            jnp.where(low_half, ph, lanes_roll(from_up, 4)),
        )
        left = (
            jnp.where(low_half, from_down, pe),
            jnp.where(low_half, lanes_roll(from_down, -4), ph),
        )
        for half in range(2):
            for c in range(3):
                strip0[3 * half + c, zi] = jnp.where(
                    lane < 64,
                    lanes_roll(right[half], -40 * c),
                    lanes_roll(left[half], 64 - 40 * c),
                )
        for c in range(2):
            a = lanes_roll(inject_a[z], 6 - 4 * c - r)
            b = lanes_roll(inject_b[z], 1 - 4 * c - r)
            strip_j[c, zi] = jnp.where(place == 6, a, jnp.where(place == 1, b, zero))

    loads[0].wait()
    loads[1].wait()

    def first_chunk(q, carry):
        for i in range(CH):
            pack(q * CH + i, q * CH + i + PAD, q * CH + i)
        send(q, 0)
        return carry

    lax.fori_loop(0, chunks, first_chunk, 0)

    loads[2].wait()

    def couple(z, carry):
        zi = z + PAD
        for xt in range(TILES):
            label = labels[zi, tile_rows(xt), :]
            value = zero
            for n in range(4):
                value = jnp.where(label == n, 0.5 * inverse[n], value)
            coup[zi, tile_rows(xt), :] = value
        return carry

    lax.fori_loop(0, nz, couple, 0)

    def c_copy(d, arriving):
        lower = (d == 0) == arriving
        src = coup.at[planes, pl.ds(TOP + 4 if d == 0 else TOP + 32, 4), :]
        dst = c_recv.at[:, pl.ds(0 if lower else 4, 4), :]
        return remote(src, dst, c_ssem.at[d], c_rsem.at[d if arriving else OPPOSITE[d]], d)

    for d in range(2):
        start_if(d, c_copy(d, False))

    total = w_send[...]
    for j in range(1, n_gx):
        w_copy(j, j, j).wait()
        total = total + w_all[j]
    loads[3].wait()
    for d in range(2):
        @pl.when(exists[d])
        def _():
            p_copy(d).wait_send()
            p_wait(d).wait_recv()
    parts = []
    for c in range(2):
        for g in range(4):
            keep = (lane < 32) & (lax.rem(lane // 4, 2) == c)
            parts.append(jnp.where(keep, lanes_roll(total, -32 * g), zero))
    weights = jnp.concatenate(parts, axis=0)
    first = start[0]
    last = start[0] + length[0]
    for xt in range(TILES):
        cells = pl.ds(8 * nz * xt, 8 * nz)
        now = lax.dot_general(
            profile[:, cells], weights, (((0,), (0,)), ((), ())),
            precision=HIGHEST, preferred_element_type=f32,
        )
        x = gx * 32 - 4 + 8 * xt + lax.broadcasted_iota(jnp.int32, (8 * nz, 128), 0) // nz
        j_flat[cells, :] = jnp.where((x >= first) & (x < last), now, 0.0)

    for d in range(2):
        wait_if(d, c_copy(d, True))
    where_at = offset[0]
    pick_row = lax.broadcasted_iota(jnp.int32, (128, 256), 0)
    pick_lane = lax.broadcasted_iota(jnp.int32, (128, 256), 1)
    pick_part = pick_row // 32
    pick_c = pick_lane // 128
    for t in range(TICKS):
        wanted = 8 * (t % K) + t // K + 4 * pick_c
        hit = (pick_row - 32 * pick_part == wanted) & (pick_row < 96)
        hit = hit & (pick_lane - 128 * pick_c == where_at)
        pick[t] = jnp.where(hit, 1.0, 0.0).astype(jnp.bfloat16)

    def prepare(z, carry):
        zi = z + PAD
        halo = c_recv[z]
        coup[zi, tile_rows(0), :] = jnp.where(sub < 4, halo, coup[zi, tile_rows(0), :])
        coup[zi, tile_rows(4), :] = jnp.where(sub < 4, coup[zi, tile_rows(4), :], halo)
        acc = zero
        j_parts = []
        for xt in range(TILES):
            v = coup[zi, tile_rows(xt), :]
            acc = jnp.where(group == xt, lanes_roll(v, 8 * xt + 4), acc)
            j = j_flat[pl.ds(z + 8 * nz * xt, 8, stride=nz), :]
            high = j.astype(jnp.bfloat16).astype(f32)
            middle = (j - high).astype(jnp.bfloat16).astype(f32)
            low = (j - high) - middle
            j_parts.append(
                jnp.where(lane < 32, high, 0.0)
                + jnp.where((lane >= 32) & (lane < 64), lanes_roll(middle, 32), 0.0)
                + jnp.where((lane >= 64) & (lane < 96), lanes_roll(low, 64), 0.0)
            )
            acc = jnp.where(group == 5 + xt, lanes_roll(j, 40 + 8 * xt), acc)
        j_all[zi] = jnp.concatenate([*j_parts, zero], axis=0).astype(jnp.bfloat16)
        v_send[0, z] = jnp.where((lane >= 40) & (where_at != 2), 0.0, acc)
        v_send[1, z] = jnp.where((lane >= 40) & (where_at != 125), 0.0, acc)
        return carry

    lax.fori_loop(0, nz, prepare, 0)

    def v_copy(d, arriving):
        return remote(
            v_send.at[d - 2], v_recv.at[(d - 2) if arriving else (3 - d)],
            v_ssem.at[d - 2], v_rsem.at[(d - 2) if arriving else (3 - d)], d,
        )

    for d in (2, 3):
        start_if(d, v_copy(d, False))
    for d in (2, 3):
        wait_if(d, v_copy(d, True))

    def finish(z, carry):
        zi = z + PAD
        own_down, own_up = v_send[0, z], v_send[1, z]
        from_down, from_up = v_recv[0, z], v_recv[1, z]
        right = jnp.where(low_half, own_up, from_up)
        left = jnp.where(low_half, from_down, own_up)
        strip_c[zi] = jnp.where(lane < 64, right, lanes_roll(left, 64))
        inject_a[z] = jnp.where(lane < 64, lanes_roll(from_up, -40), lanes_roll(own_down, 24))
        inject_b[z] = jnp.where(lane < 64, lanes_roll(own_up, -40), lanes_roll(from_down, 24))
        return carry

    lax.fori_loop(0, nz, finish, 0)
    loads[4].wait()

    outside_x = (sub < 4) & (gx == 0)
    half_first = jnp.where(outside_x, 0.0, jnp.full((8, 128), 0.5, f32))
    outside = (outside_x & ((group == 0) | (group == 8))) | (
        (lane >= 64) & low_half & (gy == 0)
    )
    half_strip = jnp.where(outside, 0.0, jnp.full((8, 128), 0.5, f32))

    def up_rows(v):
        return rows_roll(jnp.where(sub == 0, lanes_roll(v, -8), v), -1)

    def down_rows(v):
        return rows_roll(jnp.where(sub == 7, lanes_roll(v, 8), v), 1)

    def targets(s):
        if s == K - 1:
            return eh, eh, 3
        return e_at[s + 1], h_at[s + 1], 0

    def strip_step(zi, s):
        strip = strip_at[s]
        sx, sy, sz, tx, ty, tz = [strip[c, zi] for c in range(6)]
        sx_up, sy_up = strip[0, zi + 1], strip[1, zi + 1]
        sx_y, sz_y = lanes_roll(sx, -1), lanes_roll(sz, -1)
        sy_x, sz_x = up_rows(sy), up_rows(sz)
        ux = tx - half_strip * ((sz_y - sz) - (sy_up - sy))
        uy = ty - half_strip * ((sx_up - sx) - (sz_x - sz))
        uz = tz - half_strip * ((sy_x - sy) - (sx_y - sx))
        ghost_z = jnp.where(place == 4, sz, lanes_roll(ux, -62))
        ghost_x = jnp.where(place == 4, sx, lanes_roll(uz, -62))
        if s < K - 1:
            strip_new = strip_at[s + 1]
            tx_dn, ty_dn = strip_new[3, zi - 1], strip_new[4, zi - 1]
            c = strip_c[zi]
            vx = sx + c * ((uz - lanes_roll(uz, 1)) - (uy - ty_dn))
            vy = sy + c * ((ux - tx_dn) - (uz - down_rows(uz)))
            vz = sz + c * ((uy - down_rows(uy)) - (ux - lanes_roll(ux, 1)))
            if s == 0:
                vx = vx + strip_j[0, zi]
                vz = vz + strip_j[1, zi]
            for n, v in enumerate((vx, vy, vz, ux, uy, uz)):
                strip_new[n, zi] = v
        return [
            tuple(lanes_roll(g, 127 - (8 * xt + 4)) for g in (ghost_x, ghost_z))
            for xt in range(TILES)
        ]

    def magnetic_step(zi, s, ghosts):
        e_now, h_now = e_at[s], h_at[s]
        _, h_new, base = targets(s)
        for xt in range(TILES):
            rows = tile_rows(xt)
            above = pl.ds(TOP + 8 * xt + 1, 8)
            k = half_first if xt == 0 else 0.5
            ex, ey, ez = [e_now[n, zi, rows, :] for n in range(3)]
            hx, hy, hz = [h_now[n, zi, rows, :] for n in range(3)]
            ex_up, ey_up = e_now[0, zi + 1, rows, :], e_now[1, zi + 1, rows, :]
            ey_x, ez_x = e_now[1, zi, above, :], e_now[2, zi, above, :]
            ghost_x, ghost_z = ghosts[xt]
            ex_y = jnp.where(lane == 127, ghost_x, lanes_roll(ex, -1))
            ez_y = jnp.where(lane == 127, ghost_z, lanes_roll(ez, -1))
            h_new[base, zi, rows, :] = hx - k * ((ez_y - ez) - (ey_up - ey))
            h_new[base + 1, zi, rows, :] = hy - k * ((ex_up - ex) - (ez_x - ez))
            h_new[base + 2, zi, rows, :] = hz - k * ((ey_x - ey) - (ex_y - ex))

    def electric_step(zi, s, ghosts, sheet):
        e_now = e_at[s]
        e_new, h_new, base = targets(s)
        total = grads[s]
        around = []
        for xt in range(TILES):
            rows = tile_rows(xt)
            below = pl.ds(TOP + 8 * xt - 1, 8)
            around.append((
                [h_new[base + n, zi, rows, :] for n in range(3)],
                [h_new[base + n, zi - 1, rows, :] for n in range(2)],
                [h_new[base + n, zi, below, :] for n in range(1, 3)],
            ))
        for xt in range(TILES):
            rows = tile_rows(xt)
            (hx, hy, hz), (hx_dn, hy_dn), (hy_x, hz_x) = around[xt]
            ex, ey, ez = [e_now[n, zi, rows, :] for n in range(3)]
            ghost_z, ghost_x = ghosts[xt]
            hx_y = jnp.where(lane == 0, ghost_x, lanes_roll(hx, 1))
            hz_y = jnp.where(lane == 0, ghost_z, lanes_roll(hz, 1))
            cc = coup[zi, rows, :]
            at = slice(8 * xt, 8 * xt + 8)
            ex = ex + cc * ((hz - hz_y) - (hy - hy_dn)) + sheet[at, :128]
            ey = ey + cc * ((hx - hx_dn) - (hz - hz_x))
            ez = ez + cc * ((hy - hy_x) - (hx - hx_y)) + sheet[at, 128:]
            e_new[0, zi, rows, :] = ex
            e_new[1, zi, rows, :] = ey
            e_new[2, zi, rows, :] = ez
            total[zi, rows, :] = total[zi, rows, :] + (
                ex * fwd[0, zi, rows, :] + ey * fwd[1, zi, rows, :] + ez * fwd[2, zi, rows, :]
            )

    def stores(q):
        z0 = pl.multiple_of(q * CH, CH)
        zs = pl.ds(z0 + PAD, CH)
        out = pl.ds(z0, CH)
        return (
            pltpu.make_async_copy(
                eh.at[pl.ds(0, 3), zs, own_rows, :], e_out.at[:, out], out_sem.at[0, q]
            ),
            pltpu.make_async_copy(
                eh.at[pl.ds(3, 3), zs, own_rows, :], h_out.at[:, out], out_sem.at[1, q]
            ),
            pltpu.make_async_copy(
                grad0.at[zs, own_rows, :], g_out.at[out], out_sem.at[2, q]
            ),
        )

    cells = ROUNDS * nz

    def spot(at):
        valid = jnp.logical_and(at >= 0, at < cells)
        at = jnp.clip(at, 0, cells - 1)
        z = lax.rem(at, nz)
        return valid, at // nz, z, jnp.where(valid, z + PAD, nz + PAD + 2)

    def wave(w):
        valid, _, z, zi = spot(w - 9)
        pack(z, zi, jnp.where(valid, z, nz))
        order = tuple(reversed(range(K)))
        spots = {s: spot(w - 2 - 2 * s) for s in order}
        sheets = {}
        ghosts = {}
        for s in order:
            _, r, _, zi = spots[s]
            sheets[s] = jnp.dot(j_all[zi], pick[r * K + s], preferred_element_type=f32)
            ghosts[s] = strip_step(zi, s)
        for s in order:
            magnetic_step(spots[s][3], s, ghosts[s])
        for s in order:
            electric_step(spots[s][3], s, ghosts[s], sheets[s])
        valid, r, z, zi = spot(w)
        unpack(z, zi, lax.rem(r, 2), r)

    def one_chunk(n, carry):
        r = n // chunks
        q = n - r * chunks

        @pl.when(r < ROUNDS)
        def _():
            for d in range(8):
                wait_if(d, message(d, q, lax.rem(r, 2), True))

        def waves(i, carry):
            wave(n * CH + i)

            @pl.when(i == 0)
            def _():
                done = n - 3
                done_r = (done + chunks) // chunks
                done_q = lax.rem(done + chunks, chunks)

                @pl.when(jnp.logical_and(done >= 0, done_r < ROUNDS))
                def _():
                    send(done_q, lax.rem(done_r, 2))

                @pl.when(done_r == ROUNDS)
                def _():
                    for j in range(CH):
                        zi = done_q * CH + j + PAD
                        for xt in range(TILES):
                            rows = tile_rows(xt)
                            grad0[zi, rows, :] = (grad0[zi, rows, :] + grad1[zi, rows, :]) + (
                                grad2[zi, rows, :] + grad3[zi, rows, :]
                            )
                    for store in stores(done_q):
                        store.start()

            return carry

        return lax.fori_loop(0, CH, waves, carry)

    lax.fori_loop(0, ROUNDS * chunks + 3, one_chunk, 0)

    def finish_stores(q, carry):
        for store in stores(q):
            store.wait()
        return carry

    lax.fori_loop(0, chunks, finish_stores, 0)


def shards(n_gx, n_gy, *args):
    (electric, magnetic, forward_field, material, inv_permittivity, spectral_rate,
     intersection_partial, mode_profile, sheet_offset, plane_start, monitor_length) = args
    nz = electric.shape[1]
    f32 = jnp.float32
    zp = nz + PAD + EXTRA
    chunks = nz // CH
    dma = pltpu.SemaphoreType.DMA
    vmem = lambda *shape: pltpu.VMEM(shape, f32)
    anyspace = pl.BlockSpec(memory_space=pl.ANY)
    smem = pl.BlockSpec(memory_space=pltpu.SMEM)
    vm = pl.BlockSpec(memory_space=pltpu.VMEM)
    e, h, g = pl.pallas_call(
        functools.partial(kernel, n_gx, n_gy, nz),
        out_shape=[
            jax.ShapeDtypeStruct(electric.shape, f32),
            jax.ShapeDtypeStruct(electric.shape, f32),
            jax.ShapeDtypeStruct(material.shape, f32),
        ],
        in_specs=[anyspace, anyspace, anyspace, anyspace, smem, vm, vm, anyspace, smem, smem, smem],
        out_specs=[anyspace] * 3,
        scratch_shapes=[
            vmem(6, zp, ROWS, 128),
            *[vmem(3, zp, ROWS, 128) for _ in range(2 * K)],
            *[vmem(6, zp, 8, 128) for _ in range(K)],
            *[vmem(zp, ROWS, 128) for _ in range(K)],
            vmem(zp, ROWS, 128),
            vmem(3, zp, ROWS, 128),
            pltpu.VMEM((zp, ROWS, 128), jnp.int32),
            vmem(zp, 8, 128),
            vmem(2, zp, 8, 128),
            vmem(2, nz + CH, 8, 128),
            vmem(2, nz + CH, 8, 128),
            vmem(2, chunks + 1, 8, 128),
            vmem(2, 6, nz, 8, 128),
            vmem(2, 2, nz, 8, 128),
            vmem(2, 2, chunks, 8, 128),
            vmem(8, 128),
            vmem(n_gx, 8, 128),
            vmem(64, 40 * nz),
            vmem(40 * nz, 128),
            pltpu.VMEM((zp, 48, 128), jnp.bfloat16),
            pltpu.VMEM((TICKS, 128, 256), jnp.bfloat16),
            vmem(2, nz, 8, 128),
            vmem(2, nz, 8, 128),
            vmem(nz, 8, 128),
            vmem(nz, 8, 128),
            vmem(nz, 8, 128),
            dma((6,)),
            dma((3, chunks)),
            dma((8, chunks)),
            dma((2, 8, chunks)),
            dma((n_gx,)),
            dma((n_gx,)),
            dma((2,)),
            dma((2,)),
            dma((2,)),
            dma((2,)),
            dma((2,)),
            dma((2,)),
        ],
        compiler_params=pltpu.CompilerParams(
            collective_id=0, has_side_effects=True, vmem_limit_bytes=56 << 20
        ),
    )(
        electric, magnetic, forward_field, material, inv_permittivity,
        spectral_rate.reshape(1, -1), intersection_partial,
        mode_profile.reshape(-1, mode_profile.shape[2]),
        sheet_offset, plane_start, monitor_length,
    )
    return e, h, g * (1.0 / TICKS)


def solution(mesh):
    placed = (
        P(None, None, "gx", "gy"),
        P(None, None, "gx", "gy"),
        P(None, None, "gx", "gy"),
        P(None, "gx", "gy"),
        P(),
        P(),
        P("gx", "gy", None),
        P("gy", None, "gx"),
        P("gy"),
        P("gy"),
        P("gy"),
    )
    return jax.shard_map(
        functools.partial(shards, mesh.shape["gx"], mesh.shape["gy"]),
        mesh=mesh,
        in_specs=placed,
        out_specs=(P(None, None, "gx", "gy"), P(None, None, "gx", "gy"), P(None, "gx", "gy")),
        check_vma=False,
    )
```

```python
import functools

import jax
import jax.numpy as jnp
from jax import lax
from jax.experimental import pallas as pl
from jax.experimental.pallas import tpu as pltpu
from jax.sharding import PartitionSpec as P

MESH = pl.DeviceIdType.MESH
TICKS = 16
K = 4
ROUNDS = TICKS // K
CH = 4
BLOCK = 8
TILES = 5
TOP = 8
ROWS = 56
PAD = 1
EXTRA = 5
HIGHEST = lax.Precision.HIGHEST

DIRS = ((-1, 0), (1, 0), (0, -1), (0, 1), (-1, -1), (1, -1), (-1, 1), (1, 1))
OPPOSITE = (1, 0, 3, 2, 7, 6, 5, 4)


def lanes_roll(v, shift):
    if isinstance(shift, int):
        shift = shift % 128
        return v if shift == 0 else pltpu.roll(v, shift, 1)
    return pltpu.roll(v, lax.rem(shift + 256, 128), 1)


def rows_roll(v, shift):
    return pltpu.roll(v, shift % 8, 0)


def tile_rows(xt):
    return pl.ds(TOP + 8 * xt, 8)


def kernel(
    n_gx, n_gy, nz,
    e_in, h_in, f_in, material_in, inverse, rate, partial, profile_in, offset, start, length,
    e_out, h_out, g_out,
    eh, e0, h0, e1, h1, e2, h2, e3, h3, strip0, strip1, strip2, strip3,
    grad0, grad1, grad2, grad3, coup, fwd, labels, strip_c, strip_j, ghost, own_pack,
    send_y, send_c, recv_x, recv_y, recv_c,
    w_send, w_all, profile, j_flat, j_all, pick, v_send, v_recv, c_recv, inject_a, inject_b,
    load_sem, out_sem, ssem, rsem, w_ssem, w_rsem, p_ssem, p_rsem, c_ssem, c_rsem, v_ssem, v_rsem,
):
    chunks = nz // CH
    blocks = nz // BLOCK
    gx = lax.axis_index("gx")
    gy = lax.axis_index("gy")
    f32 = jnp.float32
    lane = lax.broadcasted_iota(jnp.int32, (8, 128), 1)
    sub = lax.broadcasted_iota(jnp.int32, (8, 128), 0)
    group = lane // 8
    place = lane - group * 8
    low_half = place < 4
    zero = jnp.zeros((8, 128), f32)
    own_rows = pl.ds(TOP + 4, 32)

    exists = []
    devices = []
    for dx, dy in DIRS:
        ok = None
        for d, p, n in ((dx, gx, n_gx), (dy, gy, n_gy)):
            if d:
                here = (p > 0) if d < 0 else (p < n - 1)
                ok = here if ok is None else jnp.logical_and(ok, here)
        exists.append(ok)
        devices.append((gx + dx, gy + dy))

    barrier = pltpu.get_barrier_semaphore()
    for j in range(1, n_gx):
        peer = (lax.rem(gx + j, n_gx), gy)
        pl.semaphore_signal(barrier, inc=1, device_id=peer, device_id_type=MESH)
    for d in range(2, 8):
        @pl.when(exists[d])
        def _():
            pl.semaphore_signal(barrier, inc=1, device_id=devices[d], device_id_type=MESH)
    e_at = (e0, e1, e2, e3)
    h_at = (h0, h1, h2, h3, eh)
    strip_at = (strip0, strip1, strip2, strip3)
    grads = (grad0, grad1, grad2, grad3)

    planes = pl.ds(PAD, nz)
    loads = [
        pltpu.make_async_copy(e_in, eh.at[pl.ds(0, 3), planes, own_rows, :], load_sem.at[1]),
        pltpu.make_async_copy(h_in, eh.at[pl.ds(3, 3), planes, own_rows, :], load_sem.at[2]),
        pltpu.make_async_copy(material_in, labels.at[planes, own_rows, :], load_sem.at[3]),
        pltpu.make_async_copy(profile_in, profile.at[:, pl.ds(4 * nz, 32 * nz)], load_sem.at[4]),
        pltpu.make_async_copy(f_in, fwd.at[:, planes, own_rows, :], load_sem.at[5]),
    ]
    for load in loads:
        load.start()

    for c in range(3):
        for xt in range(TILES):
            eh[3 + c, 0, tile_rows(xt), :] = zero
    for level in range(K):
        for c in range(3):
            for xt in range(TILES):
                h_at[level][c, 0, tile_rows(xt), :] = zero
                e_at[level][c, nz + PAD, tile_rows(xt), :] = zero
            strip_at[level][3 + c, 0] = zero
            strip_at[level][c, nz + PAD] = zero

    def clear(zi, carry):
        for total in grads:
            for xt in range(TILES):
                total[zi, tile_rows(xt), :] = zero
        return carry

    lax.fori_loop(PAD, nz + PAD, clear, 0, unroll=4)

    def clear_x(side):
        rows = pl.ds(4 * side, 4)
        none = jnp.zeros((4, 128), f32)

        def at(z, carry):
            for par in range(2):
                for c in range(6):
                    recv_x[par, c, z, rows, :] = none
            c_recv[z, rows, :] = none
            return carry

        lax.fori_loop(0, nz, at, 0)
        edge = jnp.zeros((64, 4 * nz), f32)
        profile[:, pl.ds(36 * nz * side, 4 * nz)] = edge

    def clear_y(side):
        def at(z, carry):
            for par in range(2):
                recv_y[par, side, z] = zero
            v_recv[side, z] = zero
            return carry

        lax.fori_loop(0, nz, at, 0)

    for side in range(2):
        @pl.when(jnp.logical_not(exists[side]))
        def _():
            clear_x(side)

        @pl.when(jnp.logical_not(exists[2 + side]))
        def _():
            clear_y(side)

    for d in range(4, 8):
        rows = pl.ds(4 if DIRS[d][0] > 0 else 0, 4)

        @pl.when(jnp.logical_not(exists[d]))
        def _():
            for par in range(2):
                for q in range(chunks):
                    recv_c[par, (d - 4) // 2, q, rows, :] = jnp.zeros((4, 128), f32)

    row = lax.broadcasted_iota(jnp.int32, (32, 128), 0)
    tick = (4 * (row - (row // 4) * 4) + row // 8).astype(f32)
    radians = tick * rate[...]
    cosine = jnp.cos(radians)
    sine = jnp.sin(radians)
    cosine = jnp.concatenate([cosine] * 4, axis=0)
    sine = jnp.concatenate([sine] * 4, axis=0)
    dims = (((1,), (1,)), ((), ()))
    term = lax.dot_general(partial[0], cosine, dims, precision=HIGHEST, preferred_element_type=f32)
    term = term - lax.dot_general(
        partial[1], sine, dims, precision=HIGHEST, preferred_element_type=f32
    )
    packed = zero
    for g in range(4):
        packed = jnp.where(lane // 32 == g, term[8 * g : 8 * g + 8], packed)
    w_send[...] = packed

    def remote(src, dst, send, recv, d):
        return pltpu.make_async_remote_copy(
            src_ref=src, dst_ref=dst, send_sem=send, recv_sem=recv,
            device_id=devices[d], device_id_type=MESH,
        )

    def start_if(d, copy):
        @pl.when(exists[d])
        def _():
            copy.start()

    def wait_if(d, copy):
        @pl.when(exists[d])
        def _():
            copy.wait()

    loads[2].wait()

    def couple(z, carry):
        zi = z + PAD
        for xt in range(TILES):
            label = labels[zi, tile_rows(xt), :]
            value = zero
            for n in range(4):
                value = jnp.where(label == n, 0.5 * inverse[n], value)
            coup[zi, tile_rows(xt), :] = value
        return carry

    lax.fori_loop(0, nz, couple, 0, unroll=4)

    def w_copy(j, slot, sem_slot):
        peer = (lax.rem(gx + j, n_gx), gy)
        return pltpu.make_async_remote_copy(
            src_ref=w_send, dst_ref=w_all.at[slot], send_sem=w_ssem.at[sem_slot],
            recv_sem=w_rsem.at[sem_slot], device_id=peer, device_id_type=MESH,
        )

    one = lambda flag: jnp.where(flag, 1, 0)
    near_x = one(exists[0]) + one(exists[1])
    near_y = one(exists[2]) + one(exists[3])
    pl.semaphore_wait(barrier, n_gx - 1 + near_y * (1 + near_x))

    for j in range(1, n_gx):
        w_copy(j, j, j).start()

    def p_copy(d):
        src = profile_in.at[:, pl.ds(0 if d == 0 else 28 * nz, 4 * nz)]
        dst = profile.at[:, pl.ds(36 * nz if d == 0 else 0, 4 * nz)]
        return remote(src, dst, p_ssem.at[d], p_rsem.at[OPPOSITE[d]], d)

    def p_wait(d):
        src = profile_in.at[:, pl.ds(0, 4 * nz)]
        dst = profile.at[:, pl.ds(0 if d == 0 else 36 * nz, 4 * nz)]
        return remote(src, dst, p_ssem.at[d], p_rsem.at[d], d)

    for d in range(2):
        start_if(d, p_copy(d))

    def c_copy(d, arriving):
        lower = (d == 0) == arriving
        src = coup.at[planes, pl.ds(TOP + 4 if d == 0 else TOP + 32, 4), :]
        dst = c_recv.at[:, pl.ds(0 if lower else 4, 4), :]
        return remote(src, dst, c_ssem.at[d], c_rsem.at[d if arriving else OPPOSITE[d]], d)

    for d in range(2):
        start_if(d, c_copy(d, False))

    def message(d, q, par, arriving):
        z0 = pl.multiple_of(q * BLOCK, BLOCK)
        zs = pl.ds(z0, BLOCK)
        sem = rsem.at[par, d if arriving else OPPOSITE[d], q]
        if d < 2:
            lower = (d == 0) == arriving
            dst = recv_x.at[par, :, zs, pl.ds(0 if lower else 4, 4), :]
            src = eh.at[:, pl.ds(z0 + PAD, BLOCK), pl.ds(TOP + 4 if d == 0 else TOP + 32, 4), :]
        elif d < 4:
            dst = recv_y.at[par, (d - 2) if arriving else (3 - d), zs]
            src = send_y.at[d - 2, zs]
        else:
            side = (d - 4) // 2
            dx = DIRS[d][0]
            out = pl.ds(4 if dx < 0 else 0, 4)
            into = pl.ds(4 if (dx > 0) == arriving else 0, 4)
            corners = pl.ds(q * (BLOCK // CH), BLOCK // CH)
            dst = recv_c.at[par, side if arriving else 1 - side, corners, into, :]
            src = send_c.at[side, corners, out, :]
        return remote(src, dst, ssem.at[d, q], sem, d)

    def pack_half(zi, slot, half):
        acc = zero
        for c in range(3):
            for xt in range(TILES):
                v = eh[3 * half + c, zi, tile_rows(xt), :]
                acc = jnp.where(group == 5 * c + xt, lanes_roll(v, 40 * c + 8 * xt + 4), acc)
        own_pack[half, slot] = acc
        return acc

    def pack_sides(z, slot, pe, ph):
        i = lax.rem(z, CH)
        down = jnp.where(low_half, lanes_roll(ph, -4), pe)
        up = jnp.where(low_half, pe, lanes_roll(ph, 4))
        here = (group == i) | (group == 5 + i) | (group == 10 + i)
        for side, v in ((0, down), (1, up)):
            send_y[side, slot] = v
            moved = jnp.where(sub < 4, lanes_roll(v, 8 * i + 96), lanes_roll(v, 8 * i))
            q = slot // CH
            send_c[side, q] = jnp.where(here, moved, send_c[side, q])

    def pack(z, zi, slot):
        pack_sides(z, slot, pack_half(zi, slot, 0), pack_half(zi, slot, 1))

    def send(q, par):
        for d in range(8):
            start_if(d, message(d, q, par, False))

    xt0 = ((group == 0) | (group == 5) | (group == 10)) & (sub < 4)
    xt4 = ((group == 4) | (group == 9) | (group == 14)) & (sub >= 4)

    def unpack_tiles(z, zi, par):
        for half in range(2):
            new = (e0, h0)[half]
            for c in range(3):
                v = recv_x[par, 3 * half + c, z]
                for xt in range(TILES):
                    old = eh[3 * half + c, z + PAD, tile_rows(xt), :]
                    if xt == 0:
                        old = jnp.where(sub < 4, v, old)
                    elif xt == 4:
                        old = jnp.where(sub < 4, old, v)
                    new[c, zi, tile_rows(xt), :] = old

    def unpack_strips(z, zi, par, r):
        i = lax.rem(z, CH)
        q = z // CH
        packs = []
        for half in range(2):
            edge = zero
            for c in range(3):
                v = recv_x[par, 3 * half + c, z]
                edge = jnp.where(group == 5 * c, lanes_roll(v, 40 * c + 4), edge)
            acc = jnp.where(xt0, edge, own_pack[half, z])
            packs.append(jnp.where(xt4, lanes_roll(edge, 32), acc))
        pe, ph = packs
        sides = []
        for side in range(2):
            v = recv_y[par, side, z]
            x = recv_c[par, side, q]
            v = jnp.where(xt0, lanes_roll(x, 128 - 8 * i), v)
            v = jnp.where(xt4, lanes_roll(x, 32 - 8 * i), v)
            sides.append(v)
        from_down, from_up = sides
        right = (
            jnp.where(low_half, pe, from_up),
            jnp.where(low_half, ph, lanes_roll(from_up, 4)),
        )
        left = (
            jnp.where(low_half, from_down, pe),
            jnp.where(low_half, lanes_roll(from_down, -4), ph),
        )
        for half in range(2):
            for c in range(3):
                strip0[3 * half + c, zi] = jnp.where(
                    lane < 64,
                    lanes_roll(right[half], -40 * c),
                    lanes_roll(left[half], 64 - 40 * c),
                )
        for c in range(2):
            a = lanes_roll(inject_a[z], 6 - 4 * c - r)
            b = lanes_roll(inject_b[z], 1 - 4 * c - r)
            strip_j[c, zi] = jnp.where(place == 6, a, jnp.where(place == 1, b, zero))

    loads[0].wait()
    loads[1].wait()

    def first_block(q, carry):
        def first(i, carry):
            for j in range(CH):
                z = q * BLOCK + i * CH + j
                pack(z, z + PAD, z)
            return carry

        lax.fori_loop(0, BLOCK // CH, first, 0)

        @pl.when(q < blocks // 2)
        def _():
            send(q, 0)

        return carry

    lax.fori_loop(0, blocks, first_block, 0)

    total = w_send[...]
    for j in range(1, n_gx):
        w_copy(j, j, j).wait()
        total = total + w_all[j]
    loads[3].wait()
    for d in range(2):
        @pl.when(exists[d])
        def _():
            p_copy(d).wait_send()
            p_wait(d).wait_recv()
    parts = []
    for c in range(2):
        for g in range(4):
            keep = (lane < 32) & (lax.rem(lane // 4, 2) == c)
            parts.append(jnp.where(keep, lanes_roll(total, -32 * g), zero))
    weights = jnp.concatenate(parts, axis=0)
    first = start[0]
    last = start[0] + length[0]
    for xt in range(TILES):
        cells = pl.ds(8 * nz * xt, 8 * nz)
        now = lax.dot_general(
            profile[:, cells], weights, (((0,), (0,)), ((), ())),
            precision=HIGHEST, preferred_element_type=f32,
        )
        x = gx * 32 - 4 + 8 * xt + lax.broadcasted_iota(jnp.int32, (8 * nz, 128), 0) // nz
        j_flat[cells, :] = jnp.where((x >= first) & (x < last), now, 0.0)

    for d in range(2):
        wait_if(d, c_copy(d, True))
    where_at = offset[0]
    def prepare(z, carry):
        zi = z + PAD
        halo = c_recv[z]
        acc = zero
        for xt in range(TILES):
            v = coup[zi, tile_rows(xt), :]
            if xt == 0:
                v = jnp.where(sub < 4, halo, v)
                coup[zi, tile_rows(xt), :] = v
            elif xt == 4:
                v = jnp.where(sub < 4, v, halo)
                coup[zi, tile_rows(xt), :] = v
            acc = jnp.where(group == xt, lanes_roll(v, 8 * xt + 4), acc)
            j = j_flat[pl.ds(z + 8 * nz * xt, 8, stride=nz), :]
            acc = jnp.where(group == 5 + xt, lanes_roll(j, 40 + 8 * xt), acc)
        v_send[0, z] = jnp.where((lane >= 40) & (where_at != 2), 0.0, acc)
        v_send[1, z] = jnp.where((lane >= 40) & (where_at != 125), 0.0, acc)
        return carry

    def v_copy(d, q, arriving):
        zs = pl.ds(pl.multiple_of(q * BLOCK, BLOCK), BLOCK)
        side = (d - 2) if arriving else (3 - d)
        return remote(
            v_send.at[d - 2, zs], v_recv.at[side, zs], v_ssem.at[d - 2, q], v_rsem.at[side, q], d
        )

    def prepare_block(q, carry):
        lax.fori_loop(0, BLOCK, lambda j, c: prepare(q * BLOCK + j, c), 0, unroll=4)
        for d in (2, 3):
            start_if(d, v_copy(d, q, False))
        return carry

    lax.fori_loop(0, blocks, prepare_block, 0)

    def later_block(q, carry):
        send(q, 0)
        return carry

    lax.fori_loop(blocks // 2, blocks, later_block, 0)

    def split(z, carry):
        j_parts = []
        for xt in range(TILES):
            j = j_flat[pl.ds(z + 8 * nz * xt, 8, stride=nz), :]
            high = j.astype(jnp.bfloat16).astype(f32)
            middle = (j - high).astype(jnp.bfloat16).astype(f32)
            low = (j - high) - middle
            j_parts.append(
                jnp.where(lane < 32, high, 0.0)
                + jnp.where((lane >= 32) & (lane < 64), lanes_roll(middle, 32), 0.0)
                + jnp.where((lane >= 64) & (lane < 96), lanes_roll(low, 64), 0.0)
            )
        j_all[z + PAD] = jnp.concatenate([*j_parts, zero], axis=0).astype(jnp.bfloat16)
        return carry

    lax.fori_loop(0, nz, split, 0, unroll=4)
    pick_row = lax.broadcasted_iota(jnp.int32, (128, 256), 0)
    pick_lane = lax.broadcasted_iota(jnp.int32, (128, 256), 1)
    pick_part = pick_row // 32
    pick_c = pick_lane // 128
    for t in range(TICKS):
        wanted = 8 * (t % K) + t // K + 4 * pick_c
        hit = (pick_row - 32 * pick_part == wanted) & (pick_row < 96)
        hit = hit & (pick_lane - 128 * pick_c == where_at)
        pick[t] = jnp.where(hit, 1.0, 0.0).astype(jnp.bfloat16)

    def finish(z, carry):
        zi = z + PAD
        own_down, own_up = v_send[0, z], v_send[1, z]
        from_down, from_up = v_recv[0, z], v_recv[1, z]
        right = jnp.where(low_half, own_up, from_up)
        left = jnp.where(low_half, from_down, own_up)
        strip_c[zi] = jnp.where(lane < 64, right, lanes_roll(left, 64))
        inject_a[z] = jnp.where(lane < 64, lanes_roll(from_up, -40), lanes_roll(own_down, 24))
        inject_b[z] = jnp.where(lane < 64, lanes_roll(own_up, -40), lanes_roll(from_down, 24))
        return carry

    loads[4].wait()

    outside_x = (sub < 4) & (gx == 0)
    half_first = jnp.where(outside_x, 0.0, jnp.full((8, 128), 0.5, f32))
    outside = (outside_x & ((group == 0) | (group == 8))) | (
        (lane >= 64) & low_half & (gy == 0)
    )
    half_strip = jnp.where(outside, 0.0, jnp.full((8, 128), 0.5, f32))

    def up_rows(v):
        return rows_roll(jnp.where(sub == 0, lanes_roll(v, -8), v), -1)

    def down_rows(v):
        return rows_roll(jnp.where(sub == 7, lanes_roll(v, 8), v), 1)

    def targets(s):
        if s == K - 1:
            return eh, eh, 3
        return e_at[s + 1], h_at[s + 1], 0

    def strip_step(zi, s):
        strip = strip_at[s]
        sx, sy, sz, tx, ty, tz = [strip[c, zi] for c in range(6)]
        sx_up, sy_up = strip[0, zi + 1], strip[1, zi + 1]
        sx_y, sz_y = lanes_roll(sx, -1), lanes_roll(sz, -1)
        sy_x, sz_x = up_rows(sy), up_rows(sz)
        ux = tx - half_strip * ((sz_y - sz) - (sy_up - sy))
        uy = ty - half_strip * ((sx_up - sx) - (sz_x - sz))
        uz = tz - half_strip * ((sy_x - sy) - (sx_y - sx))
        ghost_z = jnp.where(place == 4, sz, lanes_roll(ux, -62))
        ghost_x = jnp.where(place == 4, sx, lanes_roll(uz, -62))
        if s < K - 1:
            strip_new = strip_at[s + 1]
            tx_dn, ty_dn = strip_new[3, zi - 1], strip_new[4, zi - 1]
            c = strip_c[zi]
            vx = sx + c * ((uz - lanes_roll(uz, 1)) - (uy - ty_dn))
            vy = sy + c * ((ux - tx_dn) - (uz - down_rows(uz)))
            vz = sz + c * ((uy - down_rows(uy)) - (ux - lanes_roll(ux, 1)))
            if s == 0:
                vx = vx + strip_j[0, zi]
                vz = vz + strip_j[1, zi]
            for n, v in enumerate((vx, vy, vz, ux, uy, uz)):
                strip_new[n, zi] = v
        for xt in range(TILES):
            ghost[s, xt, 0] = lanes_roll(ghost_x, 127 - (8 * xt + 4))
            ghost[s, xt, 1] = lanes_roll(ghost_z, 127 - (8 * xt + 4))

    def magnetic_step(zi, s, ghosts):
        e_now, h_now = e_at[s], h_at[s]
        _, h_new, base = targets(s)
        for xt in range(TILES):
            rows = tile_rows(xt)
            above = pl.ds(TOP + 8 * xt + 1, 8)
            k = half_first if xt == 0 else 0.5
            ex, ey, ez = [e_now[n, zi, rows, :] for n in range(3)]
            hx, hy, hz = [h_now[n, zi, rows, :] for n in range(3)]
            ex_up, ey_up = e_now[0, zi + 1, rows, :], e_now[1, zi + 1, rows, :]
            ey_x, ez_x = e_now[1, zi, above, :], e_now[2, zi, above, :]
            ghost_x, ghost_z = ghosts[xt]
            ex_y = jnp.where(lane == 127, ghost_x, lanes_roll(ex, -1))
            ez_y = jnp.where(lane == 127, ghost_z, lanes_roll(ez, -1))
            h_new[base, zi, rows, :] = hx - k * ((ez_y - ez) - (ey_up - ey))
            h_new[base + 1, zi, rows, :] = hy - k * ((ex_up - ex) - (ez_x - ez))
            h_new[base + 2, zi, rows, :] = hz - k * ((ey_x - ey) - (ex_y - ex))

    def electric_step(zi, s, ghosts, sheet):
        e_now = e_at[s]
        e_new, h_new, base = targets(s)
        total = grads[s]
        around = []
        for xt in range(TILES):
            rows = tile_rows(xt)
            below = pl.ds(TOP + 8 * xt - 1, 8)
            around.append((
                [h_new[base + n, zi, rows, :] for n in range(3)],
                [h_new[base + n, zi - 1, rows, :] for n in range(2)],
                [h_new[base + n, zi, below, :] for n in range(1, 3)],
            ))
        for xt in range(TILES):
            rows = tile_rows(xt)
            (hx, hy, hz), (hx_dn, hy_dn), (hy_x, hz_x) = around[xt]
            ex, ey, ez = [e_now[n, zi, rows, :] for n in range(3)]
            ghost_z, ghost_x = ghosts[xt]
            hx_y = jnp.where(lane == 0, ghost_x, lanes_roll(hx, 1))
            hz_y = jnp.where(lane == 0, ghost_z, lanes_roll(hz, 1))
            cc = coup[zi, rows, :]
            at = slice(8 * xt, 8 * xt + 8)
            ex = ex + cc * ((hz - hz_y) - (hy - hy_dn)) + sheet[at, :128]
            ey = ey + cc * ((hx - hx_dn) - (hz - hz_x))
            ez = ez + cc * ((hy - hy_x) - (hx - hx_y)) + sheet[at, 128:]
            e_new[0, zi, rows, :] = ex
            e_new[1, zi, rows, :] = ey
            e_new[2, zi, rows, :] = ez
            total[zi, rows, :] = total[zi, rows, :] + (
                ex * fwd[0, zi, rows, :] + ey * fwd[1, zi, rows, :] + ez * fwd[2, zi, rows, :]
            )

    def stores(q):
        z0 = pl.multiple_of(q * BLOCK, BLOCK)
        zs = pl.ds(z0 + PAD, BLOCK)
        out = pl.ds(z0, BLOCK)
        return (
            pltpu.make_async_copy(
                eh.at[pl.ds(0, 3), zs, own_rows, :], e_out.at[:, out], out_sem.at[0, q]
            ),
            pltpu.make_async_copy(
                eh.at[pl.ds(3, 3), zs, own_rows, :], h_out.at[:, out], out_sem.at[1, q]
            ),
            pltpu.make_async_copy(
                grad0.at[zs, own_rows, :], g_out.at[out], out_sem.at[2, q]
            ),
        )

    cells = ROUNDS * nz

    def spot(at):
        valid = jnp.logical_and(at >= 0, at < cells)
        at = jnp.clip(at, 0, cells - 1)
        z = lax.rem(at, nz)
        return valid, at // nz, z, jnp.where(valid, z + PAD, nz + PAD + 2)

    def wave(w):
        spots = {s: spot(w - 3 - 2 * s) for s in range(K)}
        held = {}
        sheet = {}
        p_valid, _, p_z, p_zi = spot(w - 10)
        p_slot = jnp.where(p_valid, p_z, nz)
        _, u_r, u_z, u_zi = spot(w)
        held[0] = [(ghost[0, xt, 0], ghost[0, xt, 1]) for xt in range(TILES)]
        held[3] = [(ghost[3, xt, 0], ghost[3, xt, 1]) for xt in range(TILES)]
        strip_step(spot(w - 2 - 2 * 3)[3], 3)
        held[1] = [(ghost[1, xt, 0], ghost[1, xt, 1]) for xt in range(TILES)]
        held[2] = [(ghost[2, xt, 0], ghost[2, xt, 1]) for xt in range(TILES)]
        strip_step(spot(w - 2 - 2 * 2)[3], 2)
        sheet[1] = jnp.dot(j_all[spots[1][3]], pick[spots[1][1] * K + 1], preferred_element_type=f32)
        strip_step(spot(w - 2 - 2 * 1)[3], 1)
        strip_step(spot(w - 2 - 2 * 0)[3], 0)
        half0 = pack_half(p_zi, p_slot, 0)
        magnetic_step(spots[3][3], 3, held[3])
        half1 = pack_half(p_zi, p_slot, 1)
        magnetic_step(spots[2][3], 2, held[2])
        magnetic_step(spots[1][3], 1, held[1])
        magnetic_step(spots[0][3], 0, held[0])
        electric_step(spots[1][3], 1, held[1], sheet[1])
        sheet[2] = jnp.dot(j_all[spots[2][3]], pick[spots[2][1] * K + 2], preferred_element_type=f32)
        sheet[0] = jnp.dot(j_all[spots[0][3]], pick[spots[0][1] * K + 0], preferred_element_type=f32)
        sheet[3] = jnp.dot(j_all[spots[3][3]], pick[spots[3][1] * K + 3], preferred_element_type=f32)
        electric_step(spots[0][3], 0, held[0], sheet[0])
        pack_sides(p_z, p_slot, half0, half1)
        electric_step(spots[2][3], 2, held[2], sheet[2])
        electric_step(spots[3][3], 3, held[3], sheet[3])
        unpack_strips(u_z, u_zi, lax.rem(u_r, 2), u_r)
        unpack_tiles(u_z, u_zi, lax.rem(u_r, 2))

    last_wave = cells + 10

    def one_block(n, carry):
        r = n // blocks
        q = n - r * blocks

        @pl.when(r < ROUNDS)
        def _():
            for d in range(8):
                wait_if(d, message(d, q, lax.rem(r, 2), True))

        @pl.when(n < blocks)
        def _():
            for d in (2, 3):
                wait_if(d, v_copy(d, n, True))
            lax.fori_loop(0, BLOCK, lambda j, c: finish(n * BLOCK + j, c), 0, unroll=4)

        def waves(i, carry):
            wave(n * BLOCK + i)

            @pl.when(i == 1)
            def _():
                done = n - 2
                done_r = (done + blocks) // blocks
                done_q = lax.rem(done + blocks, blocks)

                @pl.when(jnp.logical_and(done >= 0, done_r < ROUNDS))
                def _():
                    send(done_q, lax.rem(done_r, 2))

                @pl.when(done_r == ROUNDS)
                def _():
                    def add(j, carry):
                        zi = done_q * BLOCK + j + PAD
                        for xt in range(TILES):
                            rows = tile_rows(xt)
                            total = (grad0[zi, rows, :] + grad1[zi, rows, :]) + (
                                grad2[zi, rows, :] + grad3[zi, rows, :]
                            )
                            grad0[zi, rows, :] = total * (1.0 / TICKS)
                        return carry

                    lax.fori_loop(0, BLOCK, add, 0, unroll=4)
                    for store in stores(done_q):
                        store.start()

            return carry

        return lax.fori_loop(0, jnp.minimum(BLOCK, last_wave - n * BLOCK), waves, carry)

    lax.fori_loop(0, (last_wave + BLOCK - 1) // BLOCK, one_block, 0)

    def finish_stores(q, carry):
        for store in stores(q):
            store.wait()
        return carry

    lax.fori_loop(0, blocks, finish_stores, 0)


def hand_on(*refs):
    sources, targets, buffers, sems = refs[:3], refs[3:6], refs[6:9], refs[9]
    parts = [(k, c) for k in range(2) for c in range(3)] + [(2, c) for c in range(4)]
    moves = []
    for n, (k, c) in enumerate(parts):
        at = c if k < 2 else pl.ds(c * (sources[2].shape[0] // 4), sources[2].shape[0] // 4)
        moves.append((
            pltpu.make_async_copy(sources[k].at[at], buffers[k].at[at], sems.at[0, n]),
            pltpu.make_async_copy(buffers[k].at[at], targets[k].at[at], sems.at[1, n]),
        ))
    for into, _ in moves:
        into.start()
    for into, out in moves:
        into.wait()
        out.start()
    for _, out in moves:
        out.wait()


def shards(n_gx, n_gy, *args):
    (electric, magnetic, forward_field, material, inv_permittivity, spectral_rate,
     intersection_partial, mode_profile, sheet_offset, plane_start, monitor_length) = args
    nz = electric.shape[1]
    f32 = jnp.float32
    zp = nz + PAD + EXTRA
    chunks = nz // CH
    dma = pltpu.SemaphoreType.DMA
    vmem = lambda *shape: pltpu.VMEM(shape, f32)
    anyspace = pl.BlockSpec(memory_space=pl.ANY)
    smem = pl.BlockSpec(memory_space=pltpu.SMEM)
    vm = pl.BlockSpec(memory_space=pltpu.VMEM)
    e, h, g = pl.pallas_call(
        functools.partial(kernel, n_gx, n_gy, nz),
        out_shape=[
            jax.ShapeDtypeStruct(electric.shape, f32),
            jax.ShapeDtypeStruct(electric.shape, f32),
            jax.ShapeDtypeStruct(material.shape, f32),
        ],
        in_specs=[anyspace, anyspace, anyspace, anyspace, smem, vm, vm, anyspace, smem, smem, smem],
        out_specs=[anyspace] * 3,
        scratch_shapes=[
            vmem(6, zp, ROWS, 128),
            *[vmem(3, zp, ROWS, 128) for _ in range(2 * K)],
            *[vmem(6, zp, 8, 128) for _ in range(K)],
            *[vmem(zp, ROWS, 128) for _ in range(K)],
            vmem(zp, ROWS, 128),
            vmem(3, zp, ROWS, 128),
            pltpu.VMEM((zp, ROWS, 128), jnp.int32),
            vmem(zp, 8, 128),
            vmem(2, zp, 8, 128),
            vmem(K, TILES, 2, 8, 128),
            vmem(2, nz + CH, 8, 128),
            vmem(2, nz + CH, 8, 128),
            vmem(2, chunks + 1, 8, 128),
            vmem(2, 6, nz, 8, 128),
            vmem(2, 2, nz, 8, 128),
            vmem(2, 2, chunks, 8, 128),
            vmem(8, 128),
            vmem(n_gx, 8, 128),
            vmem(64, 40 * nz),
            vmem(40 * nz, 128),
            pltpu.VMEM((zp, 48, 128), jnp.bfloat16),
            pltpu.VMEM((TICKS, 128, 256), jnp.bfloat16),
            vmem(2, nz, 8, 128),
            vmem(2, nz, 8, 128),
            vmem(nz, 8, 128),
            vmem(nz, 8, 128),
            vmem(nz, 8, 128),
            dma((6,)),
            dma((3, nz // BLOCK)),
            dma((8, nz // BLOCK)),
            dma((2, 8, nz // BLOCK)),
            dma((n_gx,)),
            dma((n_gx,)),
            dma((2,)),
            dma((2,)),
            dma((2,)),
            dma((2,)),
            dma((2, nz // BLOCK)),
            dma((2, nz // BLOCK)),
        ],
        compiler_params=pltpu.CompilerParams(
            collective_id=0, has_side_effects=True, vmem_limit_bytes=56 << 20
        ),
    )(
        electric, magnetic, forward_field, material, inv_permittivity,
        spectral_rate.reshape(1, -1), intersection_partial,
        mode_profile.reshape(-1, mode_profile.shape[2]),
        sheet_offset, plane_start, monitor_length,
    )
    return pl.pallas_call(
        hand_on,
        out_shape=[jax.ShapeDtypeStruct(x.shape, f32) for x in (e, h, g)],
        in_specs=[anyspace] * 3,
        out_specs=[anyspace] * 3,
        scratch_shapes=[vmem(*x.shape) for x in (e, h, g)] + [dma((2, 10))],
    )(e, h, g)


def solution(mesh):
    placed = (
        P(None, None, "gx", "gy"),
        P(None, None, "gx", "gy"),
        P(None, None, "gx", "gy"),
        P(None, "gx", "gy"),
        P(),
        P(),
        P("gx", "gy", None),
        P("gy", None, "gx"),
        P("gy"),
        P("gy"),
        P("gy"),
    )
    return jax.shard_map(
        functools.partial(shards, mesh.shape["gx"], mesh.shape["gy"]),
        mesh=mesh,
        in_specs=placed,
        out_specs=(P(None, None, "gx", "gy"), P(None, None, "gx", "gy"), P(None, "gx", "gy")),
        check_vma=False,
    )
```

```python
import functools

import jax
import jax.numpy as jnp
from jax import lax
from jax.experimental import pallas as pl
from jax.experimental.pallas import tpu as pltpu
from jax.sharding import PartitionSpec as P

MESH = pl.DeviceIdType.MESH
TICKS = 16
K = 4
ROUNDS = TICKS // K
CH = 4
BLOCK = 4
TILES = 5
TOP = 8
ROWS = 56
PAD = 1
EXTRA = 5
HIGHEST = lax.Precision.HIGHEST

DIRS = ((-1, 0), (1, 0), (0, -1), (0, 1), (-1, -1), (1, -1), (-1, 1), (1, 1))
OPPOSITE = (1, 0, 3, 2, 7, 6, 5, 4)


def lanes_roll(v, shift):
    if isinstance(shift, int):
        shift = shift % 128
        return v if shift == 0 else pltpu.roll(v, shift, 1)
    return pltpu.roll(v, lax.rem(shift + 256, 128), 1)


def rows_roll(v, shift):
    return pltpu.roll(v, shift % 8, 0)


def tile_rows(xt):
    return pl.ds(TOP + 8 * xt, 8)


def kernel(
    n_gx, n_gy, nz,
    e_in, h_in, f_in, material_in, inverse, rate, partial, profile_in, offset, start, length,
    e_out, h_out, g_out,
    eh, e0, h0, e1, h1, e2, h2, e3, h3, strip0, strip1, strip2, strip3,
    grad0, grad1, grad2, grad3, coup, fwd, labels, strip_c, strip_j, ghost, own_pack,
    send_y, send_c, recv_x, recv_y, recv_c,
    w_send, w_all, profile, j_flat, j_all, pick, v_send, v_recv, c_recv, inject_a, inject_b,
    load_sem, out_sem, ssem, rsem, w_ssem, w_rsem, p_ssem, p_rsem, c_ssem, c_rsem, v_ssem, v_rsem,
):
    chunks = nz // CH
    blocks = nz // BLOCK
    gx = lax.axis_index("gx")
    gy = lax.axis_index("gy")
    f32 = jnp.float32
    lane = lax.broadcasted_iota(jnp.int32, (8, 128), 1)
    sub = lax.broadcasted_iota(jnp.int32, (8, 128), 0)
    group = lane // 8
    place = lane - group * 8
    low_half = place < 4
    zero = jnp.zeros((8, 128), f32)
    own_rows = pl.ds(TOP + 4, 32)

    exists = []
    devices = []
    for dx, dy in DIRS:
        ok = None
        for d, p, n in ((dx, gx, n_gx), (dy, gy, n_gy)):
            if d:
                here = (p > 0) if d < 0 else (p < n - 1)
                ok = here if ok is None else jnp.logical_and(ok, here)
        exists.append(ok)
        devices.append((gx + dx, gy + dy))

    barrier = pltpu.get_barrier_semaphore()
    for j in range(1, n_gx):
        peer = (lax.rem(gx + j, n_gx), gy)
        pl.semaphore_signal(barrier, inc=1, device_id=peer, device_id_type=MESH)
    for d in range(2, 8):
        @pl.when(exists[d])
        def _():
            pl.semaphore_signal(barrier, inc=1, device_id=devices[d], device_id_type=MESH)
    e_at = (e0, e1, e2, e3)
    h_at = (h0, h1, h2, h3, eh)
    strip_at = (strip0, strip1, strip2, strip3)
    grads = (grad0, grad1, grad2, grad3)

    planes = pl.ds(PAD, nz)
    loads = [
        pltpu.make_async_copy(e_in, eh.at[pl.ds(0, 3), planes, own_rows, :], load_sem.at[1]),
        pltpu.make_async_copy(h_in, eh.at[pl.ds(3, 3), planes, own_rows, :], load_sem.at[2]),
        pltpu.make_async_copy(material_in, labels.at[planes, own_rows, :], load_sem.at[3]),
        pltpu.make_async_copy(profile_in, profile.at[:, pl.ds(4 * nz, 32 * nz)], load_sem.at[4]),
        pltpu.make_async_copy(f_in, fwd.at[:, planes, own_rows, :], load_sem.at[5]),
    ]
    for load in loads:
        load.start()

    for c in range(3):
        for xt in range(TILES):
            eh[3 + c, 0, tile_rows(xt), :] = zero
    for level in range(K):
        for c in range(3):
            for xt in range(TILES):
                h_at[level][c, 0, tile_rows(xt), :] = zero
                e_at[level][c, nz + PAD, tile_rows(xt), :] = zero
            strip_at[level][3 + c, 0] = zero
            strip_at[level][c, nz + PAD] = zero

    def clear(zi, carry):
        for total in grads:
            for xt in range(TILES):
                total[zi, tile_rows(xt), :] = zero
        return carry

    lax.fori_loop(PAD, nz + PAD, clear, 0, unroll=4)

    def clear_x(side):
        rows = pl.ds(4 * side, 4)
        none = jnp.zeros((4, 128), f32)

        def at(z, carry):
            for par in range(2):
                for c in range(6):
                    recv_x[par, c, z, rows, :] = none
            c_recv[z, rows, :] = none
            return carry

        lax.fori_loop(0, nz, at, 0)
        edge = jnp.zeros((64, 4 * nz), f32)
        profile[:, pl.ds(36 * nz * side, 4 * nz)] = edge

    def clear_y(side):
        def at(z, carry):
            for par in range(2):
                recv_y[par, side, z] = zero
            v_recv[side, z] = zero
            return carry

        lax.fori_loop(0, nz, at, 0)

    for side in range(2):
        @pl.when(jnp.logical_not(exists[side]))
        def _():
            clear_x(side)

        @pl.when(jnp.logical_not(exists[2 + side]))
        def _():
            clear_y(side)

    for d in range(4, 8):
        rows = pl.ds(4 if DIRS[d][0] > 0 else 0, 4)

        @pl.when(jnp.logical_not(exists[d]))
        def _():
            for par in range(2):
                for q in range(chunks):
                    recv_c[par, (d - 4) // 2, q, rows, :] = jnp.zeros((4, 128), f32)

    row = lax.broadcasted_iota(jnp.int32, (32, 128), 0)
    tick = (4 * (row - (row // 4) * 4) + row // 8).astype(f32)
    radians = tick * rate[...]
    cosine = jnp.cos(radians)
    sine = jnp.sin(radians)
    cosine = jnp.concatenate([cosine] * 4, axis=0)
    sine = jnp.concatenate([sine] * 4, axis=0)
    dims = (((1,), (1,)), ((), ()))
    term = lax.dot_general(partial[0], cosine, dims, precision=HIGHEST, preferred_element_type=f32)
    term = term - lax.dot_general(
        partial[1], sine, dims, precision=HIGHEST, preferred_element_type=f32
    )
    packed = zero
    for g in range(4):
        packed = jnp.where(lane // 32 == g, term[8 * g : 8 * g + 8], packed)
    w_send[...] = packed

    def remote(src, dst, send, recv, d):
        return pltpu.make_async_remote_copy(
            src_ref=src, dst_ref=dst, send_sem=send, recv_sem=recv,
            device_id=devices[d], device_id_type=MESH,
        )

    def start_if(d, copy):
        @pl.when(exists[d])
        def _():
            copy.start()

    def wait_if(d, copy):
        @pl.when(exists[d])
        def _():
            copy.wait()

    loads[2].wait()

    def couple(z, carry):
        zi = z + PAD
        for xt in range(TILES):
            label = labels[zi, tile_rows(xt), :]
            value = zero
            for n in range(4):
                value = jnp.where(label == n, 0.5 * inverse[n], value)
            coup[zi, tile_rows(xt), :] = value
        return carry

    lax.fori_loop(0, nz, couple, 0, unroll=4)

    def w_copy(j, slot, sem_slot):
        peer = (lax.rem(gx + j, n_gx), gy)
        return pltpu.make_async_remote_copy(
            src_ref=w_send, dst_ref=w_all.at[slot], send_sem=w_ssem.at[sem_slot],
            recv_sem=w_rsem.at[sem_slot], device_id=peer, device_id_type=MESH,
        )

    one = lambda flag: jnp.where(flag, 1, 0)
    near_x = one(exists[0]) + one(exists[1])
    near_y = one(exists[2]) + one(exists[3])
    pl.semaphore_wait(barrier, n_gx - 1 + near_y * (1 + near_x))

    for j in range(1, n_gx):
        w_copy(j, j, j).start()

    def p_copy(d):
        src = profile_in.at[:, pl.ds(0 if d == 0 else 28 * nz, 4 * nz)]
        dst = profile.at[:, pl.ds(36 * nz if d == 0 else 0, 4 * nz)]
        return remote(src, dst, p_ssem.at[d], p_rsem.at[OPPOSITE[d]], d)

    def p_wait(d):
        src = profile_in.at[:, pl.ds(0, 4 * nz)]
        dst = profile.at[:, pl.ds(0 if d == 0 else 36 * nz, 4 * nz)]
        return remote(src, dst, p_ssem.at[d], p_rsem.at[d], d)

    for d in range(2):
        start_if(d, p_copy(d))

    def c_copy(d, arriving):
        lower = (d == 0) == arriving
        src = coup.at[planes, pl.ds(TOP + 4 if d == 0 else TOP + 32, 4), :]
        dst = c_recv.at[:, pl.ds(0 if lower else 4, 4), :]
        return remote(src, dst, c_ssem.at[d], c_rsem.at[d if arriving else OPPOSITE[d]], d)

    for d in range(2):
        start_if(d, c_copy(d, False))

    def message(d, q, par, arriving):
        z0 = pl.multiple_of(q * BLOCK, BLOCK)
        zs = pl.ds(z0, BLOCK)
        sem = rsem.at[par, d if arriving else OPPOSITE[d], q]
        if d < 2:
            lower = (d == 0) == arriving
            dst = recv_x.at[par, :, zs, pl.ds(0 if lower else 4, 4), :]
            src = eh.at[:, pl.ds(z0 + PAD, BLOCK), pl.ds(TOP + 4 if d == 0 else TOP + 32, 4), :]
        elif d < 4:
            dst = recv_y.at[par, (d - 2) if arriving else (3 - d), zs]
            src = send_y.at[d - 2, zs]
        else:
            side = (d - 4) // 2
            dx = DIRS[d][0]
            out = pl.ds(4 if dx < 0 else 0, 4)
            into = pl.ds(4 if (dx > 0) == arriving else 0, 4)
            corners = pl.ds(q * (BLOCK // CH), BLOCK // CH)
            dst = recv_c.at[par, side if arriving else 1 - side, corners, into, :]
            src = send_c.at[side, corners, out, :]
        return remote(src, dst, ssem.at[d, q], sem, d)

    def pack_half(zi, slot, half):
        acc = zero
        for c in range(3):
            for xt in range(TILES):
                v = eh[3 * half + c, zi, tile_rows(xt), :]
                acc = jnp.where(group == 5 * c + xt, lanes_roll(v, 40 * c + 8 * xt + 4), acc)
        own_pack[half, slot] = acc
        return acc

    def pack_sides(z, slot, pe, ph):
        i = lax.rem(z, CH)
        down = jnp.where(low_half, lanes_roll(ph, -4), pe)
        up = jnp.where(low_half, pe, lanes_roll(ph, 4))
        here = (group == i) | (group == 5 + i) | (group == 10 + i)
        for side, v in ((0, down), (1, up)):
            send_y[side, slot] = v
            moved = jnp.where(sub < 4, lanes_roll(v, 8 * i + 96), lanes_roll(v, 8 * i))
            q = slot // CH
            send_c[side, q] = jnp.where(here, moved, send_c[side, q])

    def pack(z, zi, slot):
        pack_sides(z, slot, pack_half(zi, slot, 0), pack_half(zi, slot, 1))

    def send(q, par):
        for d in range(8):
            start_if(d, message(d, q, par, False))

    xt0 = ((group == 0) | (group == 5) | (group == 10)) & (sub < 4)
    xt4 = ((group == 4) | (group == 9) | (group == 14)) & (sub >= 4)

    def unpack_tiles(z, zi, par):
        for half in range(2):
            new = (e0, h0)[half]
            for c in range(3):
                v = recv_x[par, 3 * half + c, z]
                for xt in range(TILES):
                    old = eh[3 * half + c, z + PAD, tile_rows(xt), :]
                    if xt == 0:
                        old = jnp.where(sub < 4, v, old)
                    elif xt == 4:
                        old = jnp.where(sub < 4, old, v)
                    new[c, zi, tile_rows(xt), :] = old

    def unpack_strips(z, zi, par, r):
        i = lax.rem(z, CH)
        q = z // CH
        packs = []
        for half in range(2):
            edge = zero
            for c in range(3):
                v = recv_x[par, 3 * half + c, z]
                edge = jnp.where(group == 5 * c, lanes_roll(v, 40 * c + 4), edge)
            acc = jnp.where(xt0, edge, own_pack[half, z])
            packs.append(jnp.where(xt4, lanes_roll(edge, 32), acc))
        pe, ph = packs
        sides = []
        for side in range(2):
            v = recv_y[par, side, z]
            x = recv_c[par, side, q]
            v = jnp.where(xt0, lanes_roll(x, 128 - 8 * i), v)
            v = jnp.where(xt4, lanes_roll(x, 32 - 8 * i), v)
            sides.append(v)
        from_down, from_up = sides
        right = (
            jnp.where(low_half, pe, from_up),
            jnp.where(low_half, ph, lanes_roll(from_up, 4)),
        )
        left = (
            jnp.where(low_half, from_down, pe),
            jnp.where(low_half, lanes_roll(from_down, -4), ph),
        )
        for half in range(2):
            for c in range(3):
                strip0[3 * half + c, zi] = jnp.where(
                    lane < 64,
                    lanes_roll(right[half], -40 * c),
                    lanes_roll(left[half], 64 - 40 * c),
                )
        for c in range(2):
            a = lanes_roll(inject_a[z], 6 - 4 * c - r)
            b = lanes_roll(inject_b[z], 1 - 4 * c - r)
            strip_j[c, zi] = jnp.where(place == 6, a, jnp.where(place == 1, b, zero))

    loads[0].wait()
    loads[1].wait()

    def first_block(q, carry):
        def first(i, carry):
            for j in range(CH):
                z = q * BLOCK + i * CH + j
                pack(z, z + PAD, z)
            return carry

        lax.fori_loop(0, BLOCK // CH, first, 0)

        @pl.when(q < blocks // 2)
        def _():
            send(q, 0)

        return carry

    lax.fori_loop(0, blocks, first_block, 0)

    total = w_send[...]
    for j in range(1, n_gx):
        w_copy(j, j, j).wait()
        total = total + w_all[j]
    loads[3].wait()
    for d in range(2):
        @pl.when(exists[d])
        def _():
            p_copy(d).wait_send()
            p_wait(d).wait_recv()
    parts = []
    for c in range(2):
        for g in range(4):
            keep = (lane < 32) & (lax.rem(lane // 4, 2) == c)
            parts.append(jnp.where(keep, lanes_roll(total, -32 * g), zero))
    weights = jnp.concatenate(parts, axis=0)
    first = start[0]
    last = start[0] + length[0]
    for xt in range(TILES):
        cells = pl.ds(8 * nz * xt, 8 * nz)
        now = lax.dot_general(
            profile[:, cells], weights, (((0,), (0,)), ((), ())),
            precision=HIGHEST, preferred_element_type=f32,
        )
        x = gx * 32 - 4 + 8 * xt + lax.broadcasted_iota(jnp.int32, (8 * nz, 128), 0) // nz
        j_flat[cells, :] = jnp.where((x >= first) & (x < last), now, 0.0)

    for d in range(2):
        wait_if(d, c_copy(d, True))
    where_at = offset[0]
    def prepare(z, carry):
        zi = z + PAD
        halo = c_recv[z]
        acc = zero
        for xt in range(TILES):
            v = coup[zi, tile_rows(xt), :]
            if xt == 0:
                v = jnp.where(sub < 4, halo, v)
                coup[zi, tile_rows(xt), :] = v
            elif xt == 4:
                v = jnp.where(sub < 4, v, halo)
                coup[zi, tile_rows(xt), :] = v
            acc = jnp.where(group == xt, lanes_roll(v, 8 * xt + 4), acc)
            j = j_flat[pl.ds(z + 8 * nz * xt, 8, stride=nz), :]
            acc = jnp.where(group == 5 + xt, lanes_roll(j, 40 + 8 * xt), acc)
        v_send[0, z] = jnp.where((lane >= 40) & (where_at != 2), 0.0, acc)
        v_send[1, z] = jnp.where((lane >= 40) & (where_at != 125), 0.0, acc)
        return carry

    def v_copy(d, q, arriving):
        zs = pl.ds(pl.multiple_of(q * BLOCK, BLOCK), BLOCK)
        side = (d - 2) if arriving else (3 - d)
        return remote(
            v_send.at[d - 2, zs], v_recv.at[side, zs], v_ssem.at[d - 2, q], v_rsem.at[side, q], d
        )

    def prepare_block(q, carry):
        lax.fori_loop(0, BLOCK, lambda j, c: prepare(q * BLOCK + j, c), 0, unroll=4)
        for d in (2, 3):
            start_if(d, v_copy(d, q, False))
        return carry

    lax.fori_loop(0, blocks, prepare_block, 0)

    def later_block(q, carry):
        send(q, 0)
        return carry

    lax.fori_loop(blocks // 2, blocks, later_block, 0)

    def split(z, carry):
        j_parts = []
        for xt in range(TILES):
            j = j_flat[pl.ds(z + 8 * nz * xt, 8, stride=nz), :]
            high = j.astype(jnp.bfloat16).astype(f32)
            middle = (j - high).astype(jnp.bfloat16).astype(f32)
            low = (j - high) - middle
            j_parts.append(
                jnp.where(lane < 32, high, 0.0)
                + jnp.where((lane >= 32) & (lane < 64), lanes_roll(middle, 32), 0.0)
                + jnp.where((lane >= 64) & (lane < 96), lanes_roll(low, 64), 0.0)
            )
        j_all[z + PAD] = jnp.concatenate([*j_parts, zero], axis=0).astype(jnp.bfloat16)
        return carry

    lax.fori_loop(0, nz, split, 0, unroll=4)
    pick_row = lax.broadcasted_iota(jnp.int32, (128, 256), 0)
    pick_lane = lax.broadcasted_iota(jnp.int32, (128, 256), 1)
    pick_part = pick_row // 32
    pick_c = pick_lane // 128
    for t in range(TICKS):
        wanted = 8 * (t % K) + t // K + 4 * pick_c
        hit = (pick_row - 32 * pick_part == wanted) & (pick_row < 96)
        hit = hit & (pick_lane - 128 * pick_c == where_at)
        pick[t] = jnp.where(hit, 1.0, 0.0).astype(jnp.bfloat16)

    def finish(z, carry):
        zi = z + PAD
        own_down, own_up = v_send[0, z], v_send[1, z]
        from_down, from_up = v_recv[0, z], v_recv[1, z]
        right = jnp.where(low_half, own_up, from_up)
        left = jnp.where(low_half, from_down, own_up)
        strip_c[zi] = jnp.where(lane < 64, right, lanes_roll(left, 64))
        inject_a[z] = jnp.where(lane < 64, lanes_roll(from_up, -40), lanes_roll(own_down, 24))
        inject_b[z] = jnp.where(lane < 64, lanes_roll(own_up, -40), lanes_roll(from_down, 24))
        return carry

    loads[4].wait()

    outside_x = (sub < 4) & (gx == 0)
    half_first = jnp.where(outside_x, 0.0, jnp.full((8, 128), 0.5, f32))
    outside = (outside_x & ((group == 0) | (group == 8))) | (
        (lane >= 64) & low_half & (gy == 0)
    )
    half_strip = jnp.where(outside, 0.0, jnp.full((8, 128), 0.5, f32))

    def up_rows(v):
        return rows_roll(jnp.where(sub == 0, lanes_roll(v, -8), v), -1)

    def down_rows(v):
        return rows_roll(jnp.where(sub == 7, lanes_roll(v, 8), v), 1)

    def targets(s):
        if s == K - 1:
            return eh, eh, 3
        return e_at[s + 1], h_at[s + 1], 0

    def strip_step(zi, s):
        strip = strip_at[s]
        sx, sy, sz, tx, ty, tz = [strip[c, zi] for c in range(6)]
        sx_up, sy_up = strip[0, zi + 1], strip[1, zi + 1]
        sx_y, sz_y = lanes_roll(sx, -1), lanes_roll(sz, -1)
        sy_x, sz_x = up_rows(sy), up_rows(sz)
        ux = tx - half_strip * ((sz_y - sz) - (sy_up - sy))
        uy = ty - half_strip * ((sx_up - sx) - (sz_x - sz))
        uz = tz - half_strip * ((sy_x - sy) - (sx_y - sx))
        ghost_z = jnp.where(place == 4, sz, lanes_roll(ux, -62))
        ghost_x = jnp.where(place == 4, sx, lanes_roll(uz, -62))
        if s < K - 1:
            strip_new = strip_at[s + 1]
            tx_dn, ty_dn = strip_new[3, zi - 1], strip_new[4, zi - 1]
            c = strip_c[zi]
            vx = sx + c * ((uz - lanes_roll(uz, 1)) - (uy - ty_dn))
            vy = sy + c * ((ux - tx_dn) - (uz - down_rows(uz)))
            vz = sz + c * ((uy - down_rows(uy)) - (ux - lanes_roll(ux, 1)))
            if s == 0:
                vx = vx + strip_j[0, zi]
                vz = vz + strip_j[1, zi]
            for n, v in enumerate((vx, vy, vz, ux, uy, uz)):
                strip_new[n, zi] = v
        for xt in range(TILES):
            ghost[s, xt, 0] = lanes_roll(ghost_x, 127 - (8 * xt + 4))
            ghost[s, xt, 1] = lanes_roll(ghost_z, 127 - (8 * xt + 4))

    def magnetic_step(zi, s, ghosts):
        e_now, h_now = e_at[s], h_at[s]
        _, h_new, base = targets(s)
        for xt in range(TILES):
            rows = tile_rows(xt)
            above = pl.ds(TOP + 8 * xt + 1, 8)
            k = half_first if xt == 0 else 0.5
            ex, ey, ez = [e_now[n, zi, rows, :] for n in range(3)]
            hx, hy, hz = [h_now[n, zi, rows, :] for n in range(3)]
            ex_up, ey_up = e_now[0, zi + 1, rows, :], e_now[1, zi + 1, rows, :]
            ey_x, ez_x = e_now[1, zi, above, :], e_now[2, zi, above, :]
            ghost_x, ghost_z = ghosts[xt]
            ex_y = jnp.where(lane == 127, ghost_x, lanes_roll(ex, -1))
            ez_y = jnp.where(lane == 127, ghost_z, lanes_roll(ez, -1))
            h_new[base, zi, rows, :] = hx - k * ((ez_y - ez) - (ey_up - ey))
            h_new[base + 1, zi, rows, :] = hy - k * ((ex_up - ex) - (ez_x - ez))
            h_new[base + 2, zi, rows, :] = hz - k * ((ey_x - ey) - (ex_y - ex))

    def electric_step(zi, s, ghosts, sheet):
        e_now = e_at[s]
        e_new, h_new, base = targets(s)
        total = grads[s]
        around = []
        for xt in range(TILES):
            rows = tile_rows(xt)
            below = pl.ds(TOP + 8 * xt - 1, 8)
            around.append((
                [h_new[base + n, zi, rows, :] for n in range(3)],
                [h_new[base + n, zi - 1, rows, :] for n in range(2)],
                [h_new[base + n, zi, below, :] for n in range(1, 3)],
            ))
        for xt in range(TILES):
            rows = tile_rows(xt)
            (hx, hy, hz), (hx_dn, hy_dn), (hy_x, hz_x) = around[xt]
            ex, ey, ez = [e_now[n, zi, rows, :] for n in range(3)]
            ghost_z, ghost_x = ghosts[xt]
            hx_y = jnp.where(lane == 0, ghost_x, lanes_roll(hx, 1))
            hz_y = jnp.where(lane == 0, ghost_z, lanes_roll(hz, 1))
            cc = coup[zi, rows, :]
            at = slice(8 * xt, 8 * xt + 8)
            ex = ex + cc * ((hz - hz_y) - (hy - hy_dn)) + sheet[at, :128]
            ey = ey + cc * ((hx - hx_dn) - (hz - hz_x))
            ez = ez + cc * ((hy - hy_x) - (hx - hx_y)) + sheet[at, 128:]
            e_new[0, zi, rows, :] = ex
            e_new[1, zi, rows, :] = ey
            e_new[2, zi, rows, :] = ez
            total[zi, rows, :] = total[zi, rows, :] + (
                ex * fwd[0, zi, rows, :] + ey * fwd[1, zi, rows, :] + ez * fwd[2, zi, rows, :]
            )

    def stores(q):
        z0 = pl.multiple_of(q * BLOCK, BLOCK)
        zs = pl.ds(z0 + PAD, BLOCK)
        out = pl.ds(z0, BLOCK)
        return (
            pltpu.make_async_copy(
                eh.at[pl.ds(0, 3), zs, own_rows, :], e_out.at[:, out], out_sem.at[0, q]
            ),
            pltpu.make_async_copy(
                eh.at[pl.ds(3, 3), zs, own_rows, :], h_out.at[:, out], out_sem.at[1, q]
            ),
            pltpu.make_async_copy(
                grad0.at[zs, own_rows, :], g_out.at[out], out_sem.at[2, q]
            ),
        )

    cells = ROUNDS * nz

    def spot(at):
        valid = jnp.logical_and(at >= 0, at < cells)
        at = jnp.clip(at, 0, cells - 1)
        z = lax.rem(at, nz)
        return valid, at // nz, z, jnp.where(valid, z + PAD, nz + PAD + 2)

    def wave(w):
        spots = {s: spot(w - 3 - 2 * s) for s in range(K)}
        held = {}
        sheet = {}
        p_valid, _, p_z, p_zi = spot(w - 10)
        p_slot = jnp.where(p_valid, p_z, nz)
        _, u_r, u_z, u_zi = spot(w)
        held[0] = [(ghost[0, xt, 0], ghost[0, xt, 1]) for xt in range(TILES)]
        held[3] = [(ghost[3, xt, 0], ghost[3, xt, 1]) for xt in range(TILES)]
        strip_step(spot(w - 2 - 2 * 3)[3], 3)
        held[1] = [(ghost[1, xt, 0], ghost[1, xt, 1]) for xt in range(TILES)]
        held[2] = [(ghost[2, xt, 0], ghost[2, xt, 1]) for xt in range(TILES)]
        strip_step(spot(w - 2 - 2 * 2)[3], 2)
        sheet[1] = jnp.dot(j_all[spots[1][3]], pick[spots[1][1] * K + 1], preferred_element_type=f32)
        strip_step(spot(w - 2 - 2 * 1)[3], 1)
        strip_step(spot(w - 2 - 2 * 0)[3], 0)
        half0 = pack_half(p_zi, p_slot, 0)
        magnetic_step(spots[3][3], 3, held[3])
        half1 = pack_half(p_zi, p_slot, 1)
        magnetic_step(spots[2][3], 2, held[2])
        magnetic_step(spots[1][3], 1, held[1])
        magnetic_step(spots[0][3], 0, held[0])
        electric_step(spots[1][3], 1, held[1], sheet[1])
        sheet[2] = jnp.dot(j_all[spots[2][3]], pick[spots[2][1] * K + 2], preferred_element_type=f32)
        sheet[0] = jnp.dot(j_all[spots[0][3]], pick[spots[0][1] * K + 0], preferred_element_type=f32)
        sheet[3] = jnp.dot(j_all[spots[3][3]], pick[spots[3][1] * K + 3], preferred_element_type=f32)
        electric_step(spots[0][3], 0, held[0], sheet[0])
        pack_sides(p_z, p_slot, half0, half1)
        electric_step(spots[2][3], 2, held[2], sheet[2])
        electric_step(spots[3][3], 3, held[3], sheet[3])
        unpack_strips(u_z, u_zi, lax.rem(u_r, 2), u_r)
        unpack_tiles(u_z, u_zi, lax.rem(u_r, 2))

    last_wave = cells + 10

    def one_block(n, carry):
        r = n // blocks
        q = n - r * blocks

        @pl.when(r < ROUNDS)
        def _():
            for d in range(8):
                wait_if(d, message(d, q, lax.rem(r, 2), True))

        @pl.when(n < blocks)
        def _():
            for d in (2, 3):
                wait_if(d, v_copy(d, n, True))
            lax.fori_loop(0, BLOCK, lambda j, c: finish(n * BLOCK + j, c), 0, unroll=4)

        def waves(i, carry):
            wave(n * BLOCK + i)

            @pl.when(i == 1)
            def _():
                done = n - 3
                done_r = (done + blocks) // blocks
                done_q = lax.rem(done + blocks, blocks)

                @pl.when(jnp.logical_and(done >= 0, done_r < ROUNDS))
                def _():
                    send(done_q, lax.rem(done_r, 2))

                @pl.when(done_r == ROUNDS)
                def _():
                    def add(j, carry):
                        zi = done_q * BLOCK + j + PAD
                        for xt in range(TILES):
                            rows = tile_rows(xt)
                            total = (grad0[zi, rows, :] + grad1[zi, rows, :]) + (
                                grad2[zi, rows, :] + grad3[zi, rows, :]
                            )
                            grad0[zi, rows, :] = total * (1.0 / TICKS)
                        return carry

                    lax.fori_loop(0, BLOCK, add, 0, unroll=4)
                    for store in stores(done_q):
                        store.start()

            return carry

        return lax.fori_loop(0, jnp.minimum(BLOCK, last_wave - n * BLOCK), waves, carry)

    lax.fori_loop(0, (last_wave + BLOCK - 1) // BLOCK, one_block, 0)

    def finish_stores(q, carry):
        for store in stores(q):
            store.wait()
        return carry

    lax.fori_loop(0, blocks, finish_stores, 0)


def hand_on(*refs):
    sources, targets, buffers, sems = refs[:3], refs[3:6], refs[6:9], refs[9]
    parts = [(k, c) for k in range(2) for c in range(3)] + [(2, c) for c in range(4)]
    moves = []
    for n, (k, c) in enumerate(parts):
        at = c if k < 2 else pl.ds(c * (sources[2].shape[0] // 4), sources[2].shape[0] // 4)
        moves.append((
            pltpu.make_async_copy(sources[k].at[at], buffers[k].at[at], sems.at[0, n]),
            pltpu.make_async_copy(buffers[k].at[at], targets[k].at[at], sems.at[1, n]),
        ))
    for into, _ in moves:
        into.start()
    for into, out in moves:
        into.wait()
        out.start()
    for _, out in moves:
        out.wait()


def shards(n_gx, n_gy, *args):
    (electric, magnetic, forward_field, material, inv_permittivity, spectral_rate,
     intersection_partial, mode_profile, sheet_offset, plane_start, monitor_length) = args
    nz = electric.shape[1]
    f32 = jnp.float32
    zp = nz + PAD + EXTRA
    chunks = nz // CH
    dma = pltpu.SemaphoreType.DMA
    vmem = lambda *shape: pltpu.VMEM(shape, f32)
    anyspace = pl.BlockSpec(memory_space=pl.ANY)
    smem = pl.BlockSpec(memory_space=pltpu.SMEM)
    vm = pl.BlockSpec(memory_space=pltpu.VMEM)
    e, h, g = pl.pallas_call(
        functools.partial(kernel, n_gx, n_gy, nz),
        out_shape=[
            jax.ShapeDtypeStruct(electric.shape, f32),
            jax.ShapeDtypeStruct(electric.shape, f32),
            jax.ShapeDtypeStruct(material.shape, f32),
        ],
        in_specs=[anyspace, anyspace, anyspace, anyspace, smem, vm, vm, anyspace, smem, smem, smem],
        out_specs=[anyspace] * 3,
        scratch_shapes=[
            vmem(6, zp, ROWS, 128),
            *[vmem(3, zp, ROWS, 128) for _ in range(2 * K)],
            *[vmem(6, zp, 8, 128) for _ in range(K)],
            *[vmem(zp, ROWS, 128) for _ in range(K)],
            vmem(zp, ROWS, 128),
            vmem(3, zp, ROWS, 128),
            pltpu.VMEM((zp, ROWS, 128), jnp.int32),
            vmem(zp, 8, 128),
            vmem(2, zp, 8, 128),
            vmem(K, TILES, 2, 8, 128),
            vmem(2, nz + CH, 8, 128),
            vmem(2, nz + CH, 8, 128),
            vmem(2, chunks + 1, 8, 128),
            vmem(2, 6, nz, 8, 128),
            vmem(2, 2, nz, 8, 128),
            vmem(2, 2, chunks, 8, 128),
            vmem(8, 128),
            vmem(n_gx, 8, 128),
            vmem(64, 40 * nz),
            vmem(40 * nz, 128),
            pltpu.VMEM((zp, 48, 128), jnp.bfloat16),
            pltpu.VMEM((TICKS, 128, 256), jnp.bfloat16),
            vmem(2, nz, 8, 128),
            vmem(2, nz, 8, 128),
            vmem(nz, 8, 128),
            vmem(nz, 8, 128),
            vmem(nz, 8, 128),
            dma((6,)),
            dma((3, nz // BLOCK)),
            dma((8, nz // BLOCK)),
            dma((2, 8, nz // BLOCK)),
            dma((n_gx,)),
            dma((n_gx,)),
            dma((2,)),
            dma((2,)),
            dma((2,)),
            dma((2,)),
            dma((2, nz // BLOCK)),
            dma((2, nz // BLOCK)),
        ],
        compiler_params=pltpu.CompilerParams(
            collective_id=0, has_side_effects=True, vmem_limit_bytes=56 << 20
        ),
    )(
        electric, magnetic, forward_field, material, inv_permittivity,
        spectral_rate.reshape(1, -1), intersection_partial,
        mode_profile.reshape(-1, mode_profile.shape[2]),
        sheet_offset, plane_start, monitor_length,
    )
    return pl.pallas_call(
        hand_on,
        out_shape=[jax.ShapeDtypeStruct(x.shape, f32) for x in (e, h, g)],
        in_specs=[anyspace] * 3,
        out_specs=[anyspace] * 3,
        scratch_shapes=[vmem(*x.shape) for x in (e, h, g)] + [dma((2, 10))],
    )(e, h, g)


def solution(mesh):
    placed = (
        P(None, None, "gx", "gy"),
        P(None, None, "gx", "gy"),
        P(None, None, "gx", "gy"),
        P(None, "gx", "gy"),
        P(),
        P(),
        P("gx", "gy", None),
        P("gy", None, "gx"),
        P("gy"),
        P("gy"),
        P("gy"),
    )
    return jax.shard_map(
        functools.partial(shards, mesh.shape["gx"], mesh.shape["gy"]),
        mesh=mesh,
        in_specs=placed,
        out_specs=(P(None, None, "gx", "gy"), P(None, None, "gx", "gy"), P(None, "gx", "gy")),
        check_vma=False,
    )
```

```python
import functools

import jax
import jax.numpy as jnp
from jax import lax
from jax.experimental import pallas as pl
from jax.experimental.pallas import tpu as pltpu
from jax.sharding import PartitionSpec as P

MESH = pl.DeviceIdType.MESH
TICKS = 16
K = 4
ROUNDS = TICKS // K
CH = 4
BLOCK = 4
TILES = 5
TOP = 8
ROWS = 56
PAD = 1
EXTRA = 5
HIGHEST = lax.Precision.HIGHEST

DIRS = ((-1, 0), (1, 0), (0, -1), (0, 1), (-1, -1), (1, -1), (-1, 1), (1, 1))
OPPOSITE = (1, 0, 3, 2, 7, 6, 5, 4)


def lanes_roll(v, shift):
    if isinstance(shift, int):
        shift = shift % 128
        return v if shift == 0 else pltpu.roll(v, shift, 1)
    return pltpu.roll(v, lax.rem(shift + 256, 128), 1)


def rows_roll(v, shift):
    return pltpu.roll(v, shift % 8, 0)


def tile_rows(xt):
    return pl.ds(TOP + 8 * xt, 8)


def kernel(
    n_gx, n_gy, nz,
    e_in, h_in, f_in, material_in, inverse, rate, partial, profile_in, offset, start, length,
    e_out, h_out, g_out,
    eh, e0, h0, e1, h1, e2, h2, e3, h3, strip0, strip1, strip2, strip3,
    grad0, grad1, grad2, grad3, coup, fwd, labels, strip_c, strip_j, ghost, own_pack,
    send_y, send_c, recv_x, recv_y, recv_c,
    w_send, w_all, profile, j_flat, j_all, pick, v_send, v_recv, c_recv, inject_a, inject_b,
    load_sem, out_sem, ssem, rsem, w_ssem, w_rsem, p_ssem, p_rsem, c_ssem, c_rsem, v_ssem, v_rsem,
):
    chunks = nz // CH
    blocks = nz // BLOCK
    gx = lax.axis_index("gx")
    gy = lax.axis_index("gy")
    f32 = jnp.float32
    lane = lax.broadcasted_iota(jnp.int32, (8, 128), 1)
    sub = lax.broadcasted_iota(jnp.int32, (8, 128), 0)
    group = lane // 8
    place = lane - group * 8
    low_half = place < 4
    zero = jnp.zeros((8, 128), f32)
    own_rows = pl.ds(TOP + 4, 32)

    exists = []
    devices = []
    for dx, dy in DIRS:
        ok = None
        for d, p, n in ((dx, gx, n_gx), (dy, gy, n_gy)):
            if d:
                here = (p > 0) if d < 0 else (p < n - 1)
                ok = here if ok is None else jnp.logical_and(ok, here)
        exists.append(ok)
        devices.append((gx + dx, gy + dy))

    barrier = pltpu.get_barrier_semaphore()
    for j in range(1, n_gx):
        peer = (lax.rem(gx + j, n_gx), gy)
        pl.semaphore_signal(barrier, inc=1, device_id=peer, device_id_type=MESH)
    for d in range(2, 8):
        @pl.when(exists[d])
        def _():
            pl.semaphore_signal(barrier, inc=1, device_id=devices[d], device_id_type=MESH)
    e_at = (e0, e1, e2, e3)
    h_at = (h0, h1, h2, h3, eh)
    strip_at = (strip0, strip1, strip2, strip3)
    grads = (grad0, grad1, grad2, grad3)

    planes = pl.ds(PAD, nz)
    loads = [
        pltpu.make_async_copy(e_in, eh.at[pl.ds(0, 3), planes, own_rows, :], load_sem.at[1]),
        pltpu.make_async_copy(h_in, eh.at[pl.ds(3, 3), planes, own_rows, :], load_sem.at[2]),
        pltpu.make_async_copy(material_in, labels.at[planes, own_rows, :], load_sem.at[3]),
        pltpu.make_async_copy(profile_in, profile.at[:, pl.ds(4 * nz, 32 * nz)], load_sem.at[4]),
        pltpu.make_async_copy(f_in, fwd.at[:, planes, own_rows, :], load_sem.at[5]),
    ]
    for load in loads:
        load.start()

    for c in range(3):
        for xt in range(TILES):
            eh[3 + c, 0, tile_rows(xt), :] = zero
    for level in range(K):
        for c in range(3):
            for xt in range(TILES):
                h_at[level][c, 0, tile_rows(xt), :] = zero
                e_at[level][c, nz + PAD, tile_rows(xt), :] = zero
            strip_at[level][3 + c, 0] = zero
            strip_at[level][c, nz + PAD] = zero

    def clear(zi, carry):
        for total in grads:
            for xt in range(TILES):
                total[zi, tile_rows(xt), :] = zero
        return carry

    lax.fori_loop(PAD, nz + PAD, clear, 0, unroll=4)

    def clear_x(side):
        rows = pl.ds(4 * side, 4)
        none = jnp.zeros((4, 128), f32)

        def at(z, carry):
            for par in range(2):
                for c in range(6):
                    recv_x[par, c, z, rows, :] = none
            c_recv[z, rows, :] = none
            return carry

        lax.fori_loop(0, nz, at, 0)
        edge = jnp.zeros((64, 4 * nz), f32)
        profile[:, pl.ds(36 * nz * side, 4 * nz)] = edge

    def clear_y(side):
        def at(z, carry):
            for par in range(2):
                recv_y[par, side, z] = zero
            v_recv[side, z] = zero
            return carry

        lax.fori_loop(0, nz, at, 0)

    for side in range(2):
        @pl.when(jnp.logical_not(exists[side]))
        def _():
            clear_x(side)

        @pl.when(jnp.logical_not(exists[2 + side]))
        def _():
            clear_y(side)

    for d in range(4, 8):
        rows = pl.ds(4 if DIRS[d][0] > 0 else 0, 4)

        @pl.when(jnp.logical_not(exists[d]))
        def _():
            for par in range(2):
                for q in range(chunks):
                    recv_c[par, (d - 4) // 2, q, rows, :] = jnp.zeros((4, 128), f32)

    row = lax.broadcasted_iota(jnp.int32, (32, 128), 0)
    tick = (4 * (row - (row // 4) * 4) + row // 8).astype(f32)
    radians = tick * rate[...]
    cosine = jnp.cos(radians)
    sine = jnp.sin(radians)
    cosine = jnp.concatenate([cosine] * 4, axis=0)
    sine = jnp.concatenate([sine] * 4, axis=0)
    dims = (((1,), (1,)), ((), ()))
    term = lax.dot_general(partial[0], cosine, dims, precision=HIGHEST, preferred_element_type=f32)
    term = term - lax.dot_general(
        partial[1], sine, dims, precision=HIGHEST, preferred_element_type=f32
    )
    packed = zero
    for g in range(4):
        packed = jnp.where(lane // 32 == g, term[8 * g : 8 * g + 8], packed)
    w_send[...] = packed

    def remote(src, dst, send, recv, d):
        return pltpu.make_async_remote_copy(
            src_ref=src, dst_ref=dst, send_sem=send, recv_sem=recv,
            device_id=devices[d], device_id_type=MESH,
        )

    def start_if(d, copy):
        @pl.when(exists[d])
        def _():
            copy.start()

    def wait_if(d, copy):
        @pl.when(exists[d])
        def _():
            copy.wait()

    loads[2].wait()

    def couple(z, carry):
        zi = z + PAD
        for xt in range(TILES):
            label = labels[zi, tile_rows(xt), :]
            value = zero
            for n in range(4):
                value = jnp.where(label == n, 0.5 * inverse[n], value)
            coup[zi, tile_rows(xt), :] = value
        return carry

    lax.fori_loop(0, nz, couple, 0, unroll=4)

    def w_copy(j, slot, sem_slot):
        peer = (lax.rem(gx + j, n_gx), gy)
        return pltpu.make_async_remote_copy(
            src_ref=w_send, dst_ref=w_all.at[slot], send_sem=w_ssem.at[sem_slot],
            recv_sem=w_rsem.at[sem_slot], device_id=peer, device_id_type=MESH,
        )

    one = lambda flag: jnp.where(flag, 1, 0)
    near_x = one(exists[0]) + one(exists[1])
    near_y = one(exists[2]) + one(exists[3])
    pl.semaphore_wait(barrier, n_gx - 1 + near_y * (1 + near_x))

    for j in range(1, n_gx):
        w_copy(j, j, j).start()

    def p_copy(d):
        src = profile_in.at[:, pl.ds(0 if d == 0 else 28 * nz, 4 * nz)]
        dst = profile.at[:, pl.ds(36 * nz if d == 0 else 0, 4 * nz)]
        return remote(src, dst, p_ssem.at[d], p_rsem.at[OPPOSITE[d]], d)

    def p_wait(d):
        src = profile_in.at[:, pl.ds(0, 4 * nz)]
        dst = profile.at[:, pl.ds(0 if d == 0 else 36 * nz, 4 * nz)]
        return remote(src, dst, p_ssem.at[d], p_rsem.at[d], d)

    for d in range(2):
        start_if(d, p_copy(d))

    def c_copy(d, arriving):
        lower = (d == 0) == arriving
        src = coup.at[planes, pl.ds(TOP + 4 if d == 0 else TOP + 32, 4), :]
        dst = c_recv.at[:, pl.ds(0 if lower else 4, 4), :]
        return remote(src, dst, c_ssem.at[d], c_rsem.at[d if arriving else OPPOSITE[d]], d)

    for d in range(2):
        start_if(d, c_copy(d, False))

    def message(d, q, par, arriving):
        z0 = pl.multiple_of(q * BLOCK, BLOCK)
        zs = pl.ds(z0, BLOCK)
        sem = rsem.at[par, d if arriving else OPPOSITE[d], q]
        if d < 2:
            lower = (d == 0) == arriving
            dst = recv_x.at[par, :, zs, pl.ds(0 if lower else 4, 4), :]
            src = eh.at[:, pl.ds(z0 + PAD, BLOCK), pl.ds(TOP + 4 if d == 0 else TOP + 32, 4), :]
        elif d < 4:
            dst = recv_y.at[par, (d - 2) if arriving else (3 - d), zs]
            src = send_y.at[d - 2, zs]
        else:
            side = (d - 4) // 2
            dx = DIRS[d][0]
            out = pl.ds(4 if dx < 0 else 0, 4)
            into = pl.ds(4 if (dx > 0) == arriving else 0, 4)
            corners = pl.ds(q * (BLOCK // CH), BLOCK // CH)
            dst = recv_c.at[par, side if arriving else 1 - side, corners, into, :]
            src = send_c.at[side, corners, out, :]
        return remote(src, dst, ssem.at[d, q], sem, d)

    def pack_half(zi, slot, half):
        acc = zero
        for c in range(3):
            for xt in range(TILES):
                v = eh[3 * half + c, zi, tile_rows(xt), :]
                acc = jnp.where(group == 5 * c + xt, lanes_roll(v, 40 * c + 8 * xt + 4), acc)
        own_pack[half, slot] = acc
        return acc

    def pack_sides(z, slot, pe, ph):
        i = lax.rem(z, CH)
        down = jnp.where(low_half, lanes_roll(ph, -4), pe)
        up = jnp.where(low_half, pe, lanes_roll(ph, 4))
        here = (group == i) | (group == 5 + i) | (group == 10 + i)
        for side, v in ((0, down), (1, up)):
            send_y[side, slot] = v
            moved = jnp.where(sub < 4, lanes_roll(v, 8 * i + 96), lanes_roll(v, 8 * i))
            q = slot // CH
            send_c[side, q] = jnp.where(here, moved, send_c[side, q])

    def pack(z, zi, slot):
        pack_sides(z, slot, pack_half(zi, slot, 0), pack_half(zi, slot, 1))

    def send(q, par):
        for d in range(8):
            start_if(d, message(d, q, par, False))

    xt0 = ((group == 0) | (group == 5) | (group == 10)) & (sub < 4)
    xt4 = ((group == 4) | (group == 9) | (group == 14)) & (sub >= 4)

    def unpack_tiles(z, zi, par):
        for half in range(2):
            new = (e0, h0)[half]
            for c in range(3):
                v = recv_x[par, 3 * half + c, z]
                for xt in range(TILES):
                    old = eh[3 * half + c, z + PAD, tile_rows(xt), :]
                    if xt == 0:
                        old = jnp.where(sub < 4, v, old)
                    elif xt == 4:
                        old = jnp.where(sub < 4, old, v)
                    new[c, zi, tile_rows(xt), :] = old

    def unpack_strips(z, zi, par, r):
        i = lax.rem(z, CH)
        q = z // CH
        packs = []
        for half in range(2):
            edge = zero
            for c in range(3):
                v = recv_x[par, 3 * half + c, z]
                edge = jnp.where(group == 5 * c, lanes_roll(v, 40 * c + 4), edge)
            acc = jnp.where(xt0, edge, own_pack[half, z])
            packs.append(jnp.where(xt4, lanes_roll(edge, 32), acc))
        pe, ph = packs
        sides = []
        for side in range(2):
            v = recv_y[par, side, z]
            x = recv_c[par, side, q]
            v = jnp.where(xt0, lanes_roll(x, 128 - 8 * i), v)
            v = jnp.where(xt4, lanes_roll(x, 32 - 8 * i), v)
            sides.append(v)
        from_down, from_up = sides
        right = (
            jnp.where(low_half, pe, from_up),
            jnp.where(low_half, ph, lanes_roll(from_up, 4)),
        )
        left = (
            jnp.where(low_half, from_down, pe),
            jnp.where(low_half, lanes_roll(from_down, -4), ph),
        )
        for half in range(2):
            for c in range(3):
                strip0[3 * half + c, zi] = jnp.where(
                    lane < 64,
                    lanes_roll(right[half], -40 * c),
                    lanes_roll(left[half], 64 - 40 * c),
                )
        for c in range(2):
            a = lanes_roll(inject_a[z], 6 - 4 * c - r)
            b = lanes_roll(inject_b[z], 1 - 4 * c - r)
            strip_j[c, zi] = jnp.where(place == 6, a, jnp.where(place == 1, b, zero))

    loads[0].wait()
    loads[1].wait()

    def first_block(q, carry):
        def first(i, carry):
            for j in range(CH):
                z = q * BLOCK + i * CH + j
                pack(z, z + PAD, z)
            return carry

        lax.fori_loop(0, BLOCK // CH, first, 0)

        @pl.when(q < blocks // 2)
        def _():
            send(q, 0)

        return carry

    lax.fori_loop(0, blocks, first_block, 0)

    total = w_send[...]
    for j in range(1, n_gx):
        w_copy(j, j, j).wait()
        total = total + w_all[j]
    loads[3].wait()
    for d in range(2):
        @pl.when(exists[d])
        def _():
            p_copy(d).wait_send()
            p_wait(d).wait_recv()
    parts = []
    for c in range(2):
        for g in range(4):
            keep = (lane < 32) & (lax.rem(lane // 4, 2) == c)
            parts.append(jnp.where(keep, lanes_roll(total, -32 * g), zero))
    weights = jnp.concatenate(parts, axis=0)
    first = start[0]
    last = start[0] + length[0]
    for xt in range(TILES):
        cells = pl.ds(8 * nz * xt, 8 * nz)
        now = lax.dot_general(
            profile[:, cells], weights, (((0,), (0,)), ((), ())),
            precision=HIGHEST, preferred_element_type=f32,
        )
        x = gx * 32 - 4 + 8 * xt + lax.broadcasted_iota(jnp.int32, (8 * nz, 128), 0) // nz
        j_flat[cells, :] = jnp.where((x >= first) & (x < last), now, 0.0)

    for d in range(2):
        wait_if(d, c_copy(d, True))
    where_at = offset[0]
    def prepare(z, carry):
        zi = z + PAD
        halo = c_recv[z]
        acc = zero
        for xt in range(TILES):
            v = coup[zi, tile_rows(xt), :]
            if xt == 0:
                v = jnp.where(sub < 4, halo, v)
                coup[zi, tile_rows(xt), :] = v
            elif xt == 4:
                v = jnp.where(sub < 4, v, halo)
                coup[zi, tile_rows(xt), :] = v
            acc = jnp.where(group == xt, lanes_roll(v, 8 * xt + 4), acc)
            j = j_flat[pl.ds(z + 8 * nz * xt, 8, stride=nz), :]
            acc = jnp.where(group == 5 + xt, lanes_roll(j, 40 + 8 * xt), acc)
        v_send[0, z] = jnp.where((lane >= 40) & (where_at != 2), 0.0, acc)
        v_send[1, z] = jnp.where((lane >= 40) & (where_at != 125), 0.0, acc)
        return carry

    def v_copy(d, q, arriving):
        zs = pl.ds(pl.multiple_of(q * BLOCK, BLOCK), BLOCK)
        side = (d - 2) if arriving else (3 - d)
        return remote(
            v_send.at[d - 2, zs], v_recv.at[side, zs], v_ssem.at[d - 2, q], v_rsem.at[side, q], d
        )

    def prepare_block(q, carry):
        lax.fori_loop(0, BLOCK, lambda j, c: prepare(q * BLOCK + j, c), 0, unroll=4)
        for d in (2, 3):
            start_if(d, v_copy(d, q, False))
        return carry

    lax.fori_loop(0, blocks, prepare_block, 0)

    def later_block(q, carry):
        send(q, 0)
        return carry

    lax.fori_loop(blocks // 2, blocks, later_block, 0)

    def split(z, carry):
        j_parts = []
        for xt in range(TILES):
            j = j_flat[pl.ds(z + 8 * nz * xt, 8, stride=nz), :]
            high = j.astype(jnp.bfloat16).astype(f32)
            middle = (j - high).astype(jnp.bfloat16).astype(f32)
            low = (j - high) - middle
            j_parts.append(
                jnp.where(lane < 32, high, 0.0)
                + jnp.where((lane >= 32) & (lane < 64), lanes_roll(middle, 32), 0.0)
                + jnp.where((lane >= 64) & (lane < 96), lanes_roll(low, 64), 0.0)
            )
        j_all[z + PAD] = jnp.concatenate([*j_parts, zero], axis=0).astype(jnp.bfloat16)
        return carry

    lax.fori_loop(0, nz, split, 0, unroll=4)
    pick_row = lax.broadcasted_iota(jnp.int32, (128, 256), 0)
    pick_lane = lax.broadcasted_iota(jnp.int32, (128, 256), 1)
    pick_part = pick_row // 32
    pick_c = pick_lane // 128
    for t in range(TICKS):
        wanted = 8 * (t % K) + t // K + 4 * pick_c
        hit = (pick_row - 32 * pick_part == wanted) & (pick_row < 96)
        hit = hit & (pick_lane - 128 * pick_c == where_at)
        pick[t] = jnp.where(hit, 1.0, 0.0).astype(jnp.bfloat16)

    def finish(z, carry):
        zi = z + PAD
        own_down, own_up = v_send[0, z], v_send[1, z]
        from_down, from_up = v_recv[0, z], v_recv[1, z]
        right = jnp.where(low_half, own_up, from_up)
        left = jnp.where(low_half, from_down, own_up)
        strip_c[zi] = jnp.where(lane < 64, right, lanes_roll(left, 64))
        inject_a[z] = jnp.where(lane < 64, lanes_roll(from_up, -40), lanes_roll(own_down, 24))
        inject_b[z] = jnp.where(lane < 64, lanes_roll(own_up, -40), lanes_roll(from_down, 24))
        return carry

    loads[4].wait()

    outside_x = (sub < 4) & (gx == 0)
    half_first = jnp.where(outside_x, 0.0, jnp.full((8, 128), 0.5, f32))
    outside = (outside_x & ((group == 0) | (group == 8))) | (
        (lane >= 64) & low_half & (gy == 0)
    )
    half_strip = jnp.where(outside, 0.0, jnp.full((8, 128), 0.5, f32))

    def up_rows(v):
        return rows_roll(jnp.where(sub == 0, lanes_roll(v, -8), v), -1)

    def down_rows(v):
        return rows_roll(jnp.where(sub == 7, lanes_roll(v, 8), v), 1)

    def targets(s):
        if s == K - 1:
            return eh, eh, 3
        return e_at[s + 1], h_at[s + 1], 0

    def strip_step(zi, s):
        strip = strip_at[s]
        sx, sy, sz, tx, ty, tz = [strip[c, zi] for c in range(6)]
        sx_up, sy_up = strip[0, zi + 1], strip[1, zi + 1]
        sx_y, sz_y = lanes_roll(sx, -1), lanes_roll(sz, -1)
        sy_x, sz_x = up_rows(sy), up_rows(sz)
        ux = tx - half_strip * ((sz_y - sz) - (sy_up - sy))
        uy = ty - half_strip * ((sx_up - sx) - (sz_x - sz))
        uz = tz - half_strip * ((sy_x - sy) - (sx_y - sx))
        ghost_z = jnp.where(place == 4, sz, lanes_roll(ux, -62))
        ghost_x = jnp.where(place == 4, sx, lanes_roll(uz, -62))
        if s < K - 1:
            strip_new = strip_at[s + 1]
            tx_dn, ty_dn = strip_new[3, zi - 1], strip_new[4, zi - 1]
            c = strip_c[zi]
            vx = sx + c * ((uz - lanes_roll(uz, 1)) - (uy - ty_dn))
            vy = sy + c * ((ux - tx_dn) - (uz - down_rows(uz)))
            vz = sz + c * ((uy - down_rows(uy)) - (ux - lanes_roll(ux, 1)))
            if s == 0:
                vx = vx + strip_j[0, zi]
                vz = vz + strip_j[1, zi]
            for n, v in enumerate((vx, vy, vz, ux, uy, uz)):
                strip_new[n, zi] = v
        for xt in range(TILES):
            ghost[s, xt, 0] = lanes_roll(ghost_x, 127 - (8 * xt + 4))
            ghost[s, xt, 1] = lanes_roll(ghost_z, 127 - (8 * xt + 4))

    def magnetic_step(zi, s, ghosts):
        e_now, h_now = e_at[s], h_at[s]
        _, h_new, base = targets(s)
        for xt in range(TILES):
            rows = tile_rows(xt)
            above = pl.ds(TOP + 8 * xt + 1, 8)
            k = half_first if xt == 0 else 0.5
            ex, ey, ez = [e_now[n, zi, rows, :] for n in range(3)]
            hx, hy, hz = [h_now[n, zi, rows, :] for n in range(3)]
            ex_up, ey_up = e_now[0, zi + 1, rows, :], e_now[1, zi + 1, rows, :]
            ey_x, ez_x = e_now[1, zi, above, :], e_now[2, zi, above, :]
            ghost_x, ghost_z = ghosts[xt]
            ex_y = jnp.where(lane == 127, ghost_x, lanes_roll(ex, -1))
            ez_y = jnp.where(lane == 127, ghost_z, lanes_roll(ez, -1))
            h_new[base, zi, rows, :] = hx - k * ((ez_y - ez) - (ey_up - ey))
            h_new[base + 1, zi, rows, :] = hy - k * ((ex_up - ex) - (ez_x - ez))
            h_new[base + 2, zi, rows, :] = hz - k * ((ey_x - ey) - (ex_y - ex))

    def electric_step(zi, s, ghosts, sheet):
        e_now = e_at[s]
        e_new, h_new, base = targets(s)
        total = grads[s]
        around = []
        for xt in range(TILES):
            rows = tile_rows(xt)
            below = pl.ds(TOP + 8 * xt - 1, 8)
            around.append((
                [h_new[base + n, zi, rows, :] for n in range(3)],
                [h_new[base + n, zi - 1, rows, :] for n in range(2)],
                [h_new[base + n, zi, below, :] for n in range(1, 3)],
            ))
        for xt in range(TILES):
            rows = tile_rows(xt)
            (hx, hy, hz), (hx_dn, hy_dn), (hy_x, hz_x) = around[xt]
            ex, ey, ez = [e_now[n, zi, rows, :] for n in range(3)]
            ghost_z, ghost_x = ghosts[xt]
            hx_y = jnp.where(lane == 0, ghost_x, lanes_roll(hx, 1))
            hz_y = jnp.where(lane == 0, ghost_z, lanes_roll(hz, 1))
            cc = coup[zi, rows, :]
            at = slice(8 * xt, 8 * xt + 8)
            ex = ex + cc * ((hz - hz_y) - (hy - hy_dn)) + sheet[at, :128]
            ey = ey + cc * ((hx - hx_dn) - (hz - hz_x))
            ez = ez + cc * ((hy - hy_x) - (hx - hx_y)) + sheet[at, 128:]
            e_new[0, zi, rows, :] = ex
            e_new[1, zi, rows, :] = ey
            e_new[2, zi, rows, :] = ez
            total[zi, rows, :] = total[zi, rows, :] + (
                ex * fwd[0, zi, rows, :] + ey * fwd[1, zi, rows, :] + ez * fwd[2, zi, rows, :]
            )

    def stores(q):
        z0 = pl.multiple_of(q * BLOCK, BLOCK)
        zs = pl.ds(z0 + PAD, BLOCK)
        out = pl.ds(z0, BLOCK)
        return (
            pltpu.make_async_copy(
                eh.at[pl.ds(0, 3), zs, own_rows, :], e_out.at[:, out], out_sem.at[0, q]
            ),
            pltpu.make_async_copy(
                eh.at[pl.ds(3, 3), zs, own_rows, :], h_out.at[:, out], out_sem.at[1, q]
            ),
            pltpu.make_async_copy(
                grad0.at[zs, own_rows, :], g_out.at[out], out_sem.at[2, q]
            ),
        )

    cells = ROUNDS * nz

    def spot(at):
        valid = jnp.logical_and(at >= 0, at < cells)
        at = jnp.clip(at, 0, cells - 1)
        z = lax.rem(at, nz)
        return valid, at // nz, z, jnp.where(valid, z + PAD, nz + PAD + 2)

    def wave(w):
        spots = {s: spot(w - 3 - 2 * s) for s in range(K)}
        held = {}
        sheet = {}
        p_valid, _, p_z, p_zi = spot(w - 10)
        p_slot = jnp.where(p_valid, p_z, nz)
        _, u_r, u_z, u_zi = spot(w)
        held[0] = [(ghost[0, xt, 0], ghost[0, xt, 1]) for xt in range(TILES)]
        held[3] = [(ghost[3, xt, 0], ghost[3, xt, 1]) for xt in range(TILES)]
        strip_step(spot(w - 2 - 2 * 3)[3], 3)
        held[1] = [(ghost[1, xt, 0], ghost[1, xt, 1]) for xt in range(TILES)]
        held[2] = [(ghost[2, xt, 0], ghost[2, xt, 1]) for xt in range(TILES)]
        strip_step(spot(w - 2 - 2 * 2)[3], 2)
        sheet[1] = jnp.dot(j_all[spots[1][3]], pick[spots[1][1] * K + 1], preferred_element_type=f32)
        strip_step(spot(w - 2 - 2 * 1)[3], 1)
        strip_step(spot(w - 2 - 2 * 0)[3], 0)
        half0 = pack_half(p_zi, p_slot, 0)
        magnetic_step(spots[3][3], 3, held[3])
        half1 = pack_half(p_zi, p_slot, 1)
        magnetic_step(spots[2][3], 2, held[2])
        magnetic_step(spots[1][3], 1, held[1])
        magnetic_step(spots[0][3], 0, held[0])
        electric_step(spots[1][3], 1, held[1], sheet[1])
        sheet[2] = jnp.dot(j_all[spots[2][3]], pick[spots[2][1] * K + 2], preferred_element_type=f32)
        sheet[0] = jnp.dot(j_all[spots[0][3]], pick[spots[0][1] * K + 0], preferred_element_type=f32)
        sheet[3] = jnp.dot(j_all[spots[3][3]], pick[spots[3][1] * K + 3], preferred_element_type=f32)
        electric_step(spots[0][3], 0, held[0], sheet[0])
        pack_sides(p_z, p_slot, half0, half1)
        electric_step(spots[2][3], 2, held[2], sheet[2])
        electric_step(spots[3][3], 3, held[3], sheet[3])
        unpack_strips(u_z, u_zi, lax.rem(u_r, 2), u_r)
        unpack_tiles(u_z, u_zi, lax.rem(u_r, 2))

    last_wave = cells + 10

    def one_block(n, carry):
        r = n // blocks
        q = n - r * blocks

        @pl.when(r < ROUNDS)
        def _():
            for d in range(8):
                wait_if(d, message(d, q, lax.rem(r, 2), True))

        @pl.when(n < blocks)
        def _():
            for d in (2, 3):
                wait_if(d, v_copy(d, n, True))
            lax.fori_loop(0, BLOCK, lambda j, c: finish(n * BLOCK + j, c), 0, unroll=4)

        def waves(i, carry):
            wave(n * BLOCK + i)

            @pl.when(i == 1)
            def _():
                done = n - 3
                done_r = (done + blocks) // blocks
                done_q = lax.rem(done + blocks, blocks)

                @pl.when(jnp.logical_and(done >= 0, done_r < ROUNDS))
                def _():
                    send(done_q, lax.rem(done_r, 2))

                @pl.when(done_r == ROUNDS)
                def _():
                    def add(j, carry):
                        zi = done_q * BLOCK + j + PAD
                        for xt in range(TILES):
                            rows = tile_rows(xt)
                            total = (grad0[zi, rows, :] + grad1[zi, rows, :]) + (
                                grad2[zi, rows, :] + grad3[zi, rows, :]
                            )
                            grad0[zi, rows, :] = total * (1.0 / TICKS)
                        return carry

                    lax.fori_loop(0, BLOCK, add, 0, unroll=4)
                    for store in stores(done_q):
                        store.start()

            return carry

        return lax.fori_loop(0, jnp.minimum(BLOCK, last_wave - n * BLOCK), waves, carry)

    lax.fori_loop(0, (last_wave + BLOCK - 1) // BLOCK, one_block, 0)

    def finish_stores(q, carry):
        for store in stores(q):
            store.wait()
        return carry

    lax.fori_loop(0, blocks, finish_stores, 0)


def hand_on(*refs):
    sources, targets, buffers, sems = refs[:3], refs[3:6], refs[6:9], refs[9]
    parts = [(k, c) for k in range(2) for c in range(3)] + [(2, c) for c in range(4)]
    moves = []
    for n, (k, c) in enumerate(parts):
        at = c if k < 2 else pl.ds(c * (sources[2].shape[0] // 4), sources[2].shape[0] // 4)
        moves.append((
            pltpu.make_async_copy(sources[k].at[at], buffers[k].at[at], sems.at[0, n]),
            pltpu.make_async_copy(buffers[k].at[at], targets[k].at[at], sems.at[1, n]),
        ))
    for into, _ in moves:
        into.start()
    for into, out in moves:
        into.wait()
        out.start()
    for _, out in moves:
        out.wait()


def shards(n_gx, n_gy, *args):
    (electric, magnetic, forward_field, material, inv_permittivity, spectral_rate,
     intersection_partial, mode_profile, sheet_offset, plane_start, monitor_length) = args
    nz = electric.shape[1]
    f32 = jnp.float32
    zp = nz + PAD + EXTRA
    chunks = nz // CH
    dma = pltpu.SemaphoreType.DMA
    vmem = lambda *shape: pltpu.VMEM(shape, f32)
    anyspace = pl.BlockSpec(memory_space=pl.ANY)
    smem = pl.BlockSpec(memory_space=pltpu.SMEM)
    vm = pl.BlockSpec(memory_space=pltpu.VMEM)
    e, h, g = pl.pallas_call(
        functools.partial(kernel, n_gx, n_gy, nz),
        out_shape=[
            jax.ShapeDtypeStruct(electric.shape, f32),
            jax.ShapeDtypeStruct(electric.shape, f32),
            jax.ShapeDtypeStruct(material.shape, f32),
        ],
        in_specs=[anyspace, anyspace, anyspace, anyspace, smem, vm, vm, anyspace, smem, smem, smem],
        out_specs=[anyspace] * 3,
        scratch_shapes=[
            vmem(6, zp, ROWS, 128),
            *[vmem(3, zp, ROWS, 128) for _ in range(2 * K)],
            *[vmem(6, zp, 8, 128) for _ in range(K)],
            *[vmem(zp, ROWS, 128) for _ in range(K)],
            vmem(zp, ROWS, 128),
            vmem(3, zp, ROWS, 128),
            pltpu.VMEM((zp, ROWS, 128), jnp.int32),
            vmem(zp, 8, 128),
            vmem(2, zp, 8, 128),
            vmem(K, TILES, 2, 8, 128),
            vmem(2, nz + CH, 8, 128),
            vmem(2, nz + CH, 8, 128),
            vmem(2, chunks + 1, 8, 128),
            vmem(2, 6, nz, 8, 128),
            vmem(2, 2, nz, 8, 128),
            vmem(2, 2, chunks, 8, 128),
            vmem(8, 128),
            vmem(n_gx, 8, 128),
            vmem(64, 40 * nz),
            vmem(41 * nz, 128),
            pltpu.VMEM((zp, 48, 128), jnp.bfloat16),
            pltpu.VMEM((TICKS, 128, 256), jnp.bfloat16),
            vmem(2, nz, 8, 128),
            vmem(2, nz, 8, 128),
            vmem(nz, 8, 128),
            vmem(nz, 8, 128),
            vmem(nz, 8, 128),
            dma((6,)),
            dma((3, nz // BLOCK)),
            dma((8, nz // BLOCK)),
            dma((2, 8, nz // BLOCK)),
            dma((n_gx,)),
            dma((n_gx,)),
            dma((2,)),
            dma((2,)),
            dma((2,)),
            dma((2,)),
            dma((2, nz // BLOCK)),
            dma((2, nz // BLOCK)),
        ],
        compiler_params=pltpu.CompilerParams(
            collective_id=0, has_side_effects=True, vmem_limit_bytes=56 << 20
        ),
    )(
        electric, magnetic, forward_field, material, inv_permittivity,
        spectral_rate.reshape(1, -1), intersection_partial,
        mode_profile.reshape(-1, mode_profile.shape[2]),
        sheet_offset, plane_start, monitor_length,
    )
    return pl.pallas_call(
        hand_on,
        out_shape=[jax.ShapeDtypeStruct(x.shape, f32) for x in (e, h, g)],
        in_specs=[anyspace] * 3,
        out_specs=[anyspace] * 3,
        scratch_shapes=[vmem(*x.shape) for x in (e, h, g)] + [dma((2, 10))],
    )(e, h, g)


def solution(mesh):
    placed = (
        P(None, None, "gx", "gy"),
        P(None, None, "gx", "gy"),
        P(None, None, "gx", "gy"),
        P(None, "gx", "gy"),
        P(),
        P(),
        P("gx", "gy", None),
        P("gy", None, "gx"),
        P("gy"),
        P("gy"),
        P("gy"),
    )
    return jax.shard_map(
        functools.partial(shards, mesh.shape["gx"], mesh.shape["gy"]),
        mesh=mesh,
        in_specs=placed,
        out_specs=(P(None, None, "gx", "gy"), P(None, None, "gx", "gy"), P(None, "gx", "gy")),
        check_vma=False,
    )
```
